32 devices in a mesh: row: 8 (over y, x, core), col: 4 (over z).
Axes of the slice: x: 2, y: 2, z: 4, core: 2. Of those that a mesh axis runs over, the one named last changes fastest.
Arguments:
- hidden: bfloat16 [4096, 2048], P('col', 'row'), may hold values from -6 to 6
- lengths: int32 [32], replicated, may hold values from 16 to 128, as said below
- square_matrix_shards: float32 [7, 2048, 2048], P(None, ('row', 'col')), may hold values from -0.125 to 0.125
- channel_mix_shards: float32 [2, 2048, 8192], P(None, ('row', 'col')), may hold values from -0.09375 to 0.09375
- lowrank_down: bfloat16 [2, 2048, 96], replicated, may hold values from -0.125 to 0.125
- lowrank_up: bfloat16 [2, 96, 2048], replicated, may hold values from -0.625 to 0.625
- token_shift_weights: float32 [9, 2048], replicated, may hold values from 0 to 1
- attention_coefficients: float32 [6, 2048], replicated, may hold values from -8 to 2, as said below
- norm_parameters: float32 [6, 2048], P(None, 'row'), may hold values from 0.25 to 1.75
Outputs:
- out_hidden: bfloat16 [4096, 2048], P('col', 'row')
- next_rkv: bfloat16 [3, 4096, 2048], P(None, 'row', 'col')
- final_state: float32 [32, 32, 4096], P('row', 'col')
The draws below stay inside these ranges and needn't reach their ends.
Inputs may be any that keep to these rules, and one draw needn't show every extreme that they name: `lengths`: every prompt length lies between 16 and 128; in every draw at least one prompt has length 128, most are under 41. `attention_coefficients`: row 0 lies in -8 to -1, row 1 in -2 to 2, row 2 in 0.5 to 1.5, row 3 in -1 to 1, row 4 in 0.5 to 1.5, row 5 in -0.5 to 0.5.
All inputs are finite; a program needn't handle non-finite values.
Results may differ from the reference program's by a relative error of at most 0.034.
Values may be sent and summed in bfloat16 or wider, within the bound.
No kernel may reach another device: no remote copies, remote signals or barrier semaphores. Data moves between devices by JAX's collectives and lax.ppermute only.
A program may use at most 128 MiB of HBM per device.

```python
import jax
import jax.numpy as jnp
from jax import lax

MODEL_WIDTH = 2048
FF = 8192
ATTENTION_DIM = 64
LOWRANK_WIDTH = 96
LMAX = 128
PROMPTS = 32
TOKENS = 4096
N_ROW = 8


def draw_lengths(key, part):
    first_key, second_key, third_key = jax.random.split(jax.random.fold_in(key, 11), 3)
    short = jnp.minimum(jax.random.randint(first_key, (PROMPTS,), 16, 41), LMAX)
    longer = jax.random.randint(second_key, (PROMPTS,), 0, 4) == 0
    picked = jax.random.randint(third_key, (), 0, PROMPTS)
    forced = jnp.arange(PROMPTS) == picked
    return jnp.where(longer | forced, LMAX, short).astype(jnp.int32)


def draw_attention_coefficients(key, part):
    unit = jax.random.uniform(jax.random.fold_in(key, 23), (6, MODEL_WIDTH), jnp.float32)
    lower = jnp.array([-8.0, -2.0, 0.5, -1.0, 0.5, -0.5], jnp.float32)
    upper = jnp.array([-1.0, 2.0, 1.5, 1.0, 1.5, 0.5], jnp.float32)
    return lower[:, None] + (upper - lower)[:, None] * unit


def level_of(stream_key, dims, cuts, smallest, high):
    level = 1.0
    for dim, blocks in cuts:
        steps = jax.random.uniform(jax.random.fold_in(jax.random.fold_in(stream_key, 6), dim), (blocks,), jnp.float32, smallest / len(cuts), high / len(cuts))
        level = level * jnp.repeat(jnp.exp(steps), dims[dim] // blocks).reshape((-1,) + (1,) * (len(dims) - 1 - dim))
    return level


def scatter_about(rng, shape, deviation, bound, shards=(), kind=jnp.bfloat16):
    factor_of = level_of(rng, shape, shards, -0.22, 0.18) if shards else 1.0
    values = jax.random.normal(rng, shape, jnp.float32) * deviation * factor_of
    return jnp.minimum(jnp.maximum(values, -bound), bound).astype(kind)


def setup_inputs(seed: int = 0) -> dict:
    key_of = jax.random.split(jax.random.key(seed), 10)
    hidden = scatter_about(key_of[0], (TOKENS, MODEL_WIDTH), 1.0, 6.0, ((0, 4), (1, 8)))
    lengths = draw_lengths(jax.random.fold_in(key_of[9], 71), 0)
    square_matrix_shards = scatter_about(key_of[2], (7, MODEL_WIDTH, MODEL_WIDTH), MODEL_WIDTH ** -0.5, 0.125, ((1, 32),), jnp.float32)
    channel_mix_shards = scatter_about(key_of[3], (2, MODEL_WIDTH, FF), (2 * MODEL_WIDTH) ** -0.5, 0.09375, ((1, 32),), jnp.float32)
    lowrank_down = scatter_about(key_of[4], (2, MODEL_WIDTH, LOWRANK_WIDTH), MODEL_WIDTH ** -0.5, 0.125)
    lowrank_up = scatter_about(key_of[5], (2, LOWRANK_WIDTH, MODEL_WIDTH), LOWRANK_WIDTH ** -0.5, 0.625)
    token_shift_weights = jnp.clip(jax.random.uniform(key_of[6], (9, MODEL_WIDTH), jnp.float32, 0.0, 1.0), 0.0, 1.0)
    attention_coefficients = draw_attention_coefficients(jax.random.fold_in(key_of[9], 71), 0)
    norm_parameters = jnp.clip(1.0 + 0.15 * jax.random.normal(key_of[8], (6, MODEL_WIDTH), jnp.float32), 0.25, 1.75)
    return dict(hidden=hidden, lengths=lengths, square_matrix_shards=square_matrix_shards, channel_mix_shards=channel_mix_shards, lowrank_down=lowrank_down, lowrank_up=lowrank_up, token_shift_weights=token_shift_weights, attention_coefficients=attention_coefficients, norm_parameters=norm_parameters)


def shifted(source):
    grid = source.reshape(-1, LMAX, source.shape[-1])
    before = jnp.concatenate([jnp.zeros_like(grid[:, :1]), grid[:, :-1]], axis=1)
    return before.reshape(source.shape)

def mixed(source, weight):
    wide = source.astype(jnp.float32)
    return (wide + (shifted(wide) - wide) * weight).astype(jnp.bfloat16)

def normed(source, gain, bias):
    width = source.shape[-1]
    center = lax.optimization_barrier(jnp.sum(source, axis=-1, keepdims=True)) / width
    second = lax.optimization_barrier(jnp.sum(source * source, axis=-1, keepdims=True)) / width
    scaled = (source - center) * lax.rsqrt(second - center * center + 1e-05)
    return (scaled * gain + bias).astype(jnp.bfloat16)

def block_product_sum(source, weight):
    width = source.shape[1] // N_ROW
    total = jnp.zeros((source.shape[0], weight.shape[1]), jnp.float32)
    for block_index in range(N_ROW):
        lower = block_index * width
        partial_sum = jnp.dot(source[:, lower:lower + width], weight[lower:lower + width], preferred_element_type=jnp.float32)
        total = total + lax.optimization_barrier(partial_sum.astype(jnp.bfloat16)).astype(jnp.float32)
    return total

def run_scan(acceptance_gate_entries, key_vecs, value_vecs, decay_logarithm, remove_dir, write_dir):
    highest = lax.Precision.HIGHEST

    def advance(state, inputs):
        rec_now, key_now, val_now, decay_now, remove_now, write_now = inputs
        pulled = jnp.einsum('phvk,phk->phv', state, remove_now, precision=highest)
        state = state * jnp.exp(decay_now)[:, :, None, :] + pulled[..., None] * write_now[:, :, None, :] + val_now[..., None] * key_now[:, :, None, :]
        output = jnp.einsum('phvk,phk->phv', state, rec_now, precision=highest)
        return (state, output)
    inputs = tuple((jnp.moveaxis(item, 1, 0) for item in (acceptance_gate_entries, key_vecs, value_vecs, decay_logarithm, remove_dir, write_dir)))
    prompts, attention_entries = (acceptance_gate_entries.shape[0], acceptance_gate_entries.shape[2])
    start = jnp.zeros((prompts, attention_entries, ATTENTION_DIM, ATTENTION_DIM), jnp.float32)
    final, result_entries = lax.scan(advance, start, inputs)
    return (final, jnp.moveaxis(result_entries, 0, 1))

def reference(hidden, lengths, square_matrix_shards, channel_mix_shards, lowrank_down, lowrank_up, token_shift_weights, attention_coefficients, norm_parameters):
    square = square_matrix_shards.astype(jnp.bfloat16)
    mlp_weights = channel_mix_shards.astype(jnp.bfloat16)
    resid = hidden.astype(jnp.float32)
    first = normed(resid, norm_parameters[0], norm_parameters[1])
    shift_blends = [mixed(first, token_shift_weights[column_step]) for column_step in range(5)]
    acceptance_gate_entries = block_product_sum(shift_blends[0], square[0])
    key_vecs = block_product_sum(shift_blends[1], square[1])
    value_vecs = block_product_sum(shift_blends[2], square[2])
    decay_lowrank = block_product_sum(shift_blends[3], lowrank_down[0])
    rate_lowrank = block_product_sum(shift_blends[4], lowrank_down[1])
    decay_input = jnp.tanh(decay_lowrank).astype(jnp.bfloat16)
    decay_logarithm = -0.606531 * jax.nn.sigmoid(attention_coefficients[0] + jnp.dot(decay_input, lowrank_up[0], preferred_element_type=jnp.float32))
    incontext_rate = jax.nn.sigmoid(attention_coefficients[1] + jnp.dot(rate_lowrank.astype(jnp.bfloat16), lowrank_up[1], preferred_element_type=jnp.float32))
    prompts = lengths.shape[0]
    attention_entries = MODEL_WIDTH // ATTENTION_DIM

    def split_heads(source):
        return source.reshape(prompts, LMAX, attention_entries, ATTENTION_DIM)
    acceptance_gate_entries = split_heads(acceptance_gate_entries)
    key_vecs = split_heads(key_vecs)
    value_vecs = split_heads(value_vecs)
    decay_logarithm = split_heads(decay_logarithm)
    incontext_rate = split_heads(incontext_rate)
    kappa = key_vecs * attention_coefficients[2].reshape(attention_entries, ATTENTION_DIM)
    kappa_hat = kappa * lax.rsqrt(lax.optimization_barrier(jnp.sum(kappa * kappa, axis=-1, keepdims=True)) + 1e-05)
    present_entries = (jnp.arange(LMAX)[None, :] < lengths[:, None]).astype(jnp.float32)[:, :, None, None]
    remove_dir = -kappa_hat * present_entries
    write_dir = kappa_hat * incontext_rate * present_entries
    present_address_vector = key_vecs * present_entries
    present_payload_vector = value_vecs * present_entries
    final, result_entries = run_scan(acceptance_gate_entries, present_address_vector, present_payload_vector, decay_logarithm * present_entries, remove_dir, write_dir)
    extra_reward_factor = lax.optimization_barrier(jnp.sum(acceptance_gate_entries * present_address_vector * attention_coefficients[3].reshape(attention_entries, ATTENTION_DIM), axis=-1, keepdims=True)) * present_payload_vector
    attention_results = (result_entries + extra_reward_factor) * present_entries
    center = lax.optimization_barrier(jnp.mean(attention_results, axis=-1, keepdims=True))
    spread = lax.optimization_barrier(jnp.mean(jnp.square(attention_results - center), axis=-1, keepdims=True))
    grouped = ((attention_results - center) * lax.rsqrt(spread + 0.00064)).reshape(prompts * LMAX, MODEL_WIDTH)
    att = (grouped * attention_coefficients[4] + attention_coefficients[5]).astype(jnp.bfloat16)
    contract = (((1,), (1,)), ((), ()))
    attn_out = lax.dot_general(att, square[3], contract, preferred_element_type=jnp.float32)
    mid = (resid + attn_out).astype(jnp.bfloat16)
    mid_wide = mid.astype(jnp.float32)
    channel_in = mixed(normed(mid_wide, norm_parameters[2], norm_parameters[3]), token_shift_weights[5])
    pre_act = jnp.dot(channel_in, mlp_weights[0], preferred_element_type=jnp.float32)
    act = jnp.square(jax.nn.relu(pre_act)).astype(jnp.bfloat16)
    channel_out = lax.dot_general(act, mlp_weights[1], contract, preferred_element_type=jnp.float32)
    out_hidden = (mid_wide + channel_out).astype(jnp.bfloat16)
    third = normed(out_hidden.astype(jnp.float32), norm_parameters[4], norm_parameters[5])
    next_rkv = jnp.stack([block_product_sum(mixed(third, token_shift_weights[6 + column_step]), square[4 + column_step]).astype(jnp.bfloat16) for column_step in range(3)])
    final_state = final.reshape(prompts, attention_entries, ATTENTION_DIM * ATTENTION_DIM)
    return (out_hidden, next_rkv, final_state)
```

```python
import functools

import jax
import jax.numpy as jnp
from jax import lax
from jax.experimental import pallas as pl
from jax.experimental.pallas import tpu as pltpu
from jax.sharding import PartitionSpec as P

LMAX = 128
HEAD = 64
F32 = jnp.float32
BF16 = jnp.bfloat16


def bdot(a, b, ca=1, cb=0):
    return lax.dot_general(
        a.astype(BF16), b.astype(BF16), (((ca,), (cb,)), ((), ())), preferred_element_type=F32
    )


def halves(x):
    top = x.astype(BF16)
    return top, (x - top.astype(F32)).astype(BF16)


def dot3(a, b, ca=1, cb=0):
    ah, al = halves(a)
    bh, bl = halves(b)
    return bdot(ah, bh, ca, cb) + (bdot(ah, bl, ca, cb) + bdot(al, bh, ca, cb))


def head_sums(x, same):
    top, low = halves(x)
    return bdot(top, same) + bdot(low, same)


def time_kernel(nb, per, lens, *refs):
    xg = refs[:nb]
    gb, shift, w, ld, lu, co, wo, out_ref, state_ref, mixes = refs[nb:]
    rows = per * LMAX
    fw = xg[0].shape[1]
    width = nb * fw
    hc = w.shape[2]
    blocks = [x[...].astype(F32) for x in xg]
    total = sum(jnp.sum(b, axis=1, keepdims=True) for b in blocks)
    square = sum(jnp.sum(b * b, axis=1, keepdims=True) for b in blocks)
    center = total / width
    scale = lax.rsqrt(square / width - center * center + 1e-05)
    first_row = lax.broadcasted_iota(jnp.int32, (rows, fw), 0) % LMAX == 0
    for i in range(nb):
        z = (xg[i][...].astype(F32) - center) * scale * gb[i : i + 1] + gb[nb + i : nb + i + 1]
        z = z.astype(BF16).astype(F32)
        step = jnp.where(first_row, 0.0, pltpu.roll(z, 1, 0)) - z
        for j in range(5):
            mixes[j, :, i * fw : (i + 1) * fw] = (z + step * shift[j * nb + i : j * nb + i + 1]).astype(BF16)
    r = bdot(mixes[0], w[0])
    k = bdot(mixes[1], w[1])
    v = bdot(mixes[2], w[2])
    dl = bdot(mixes[3], ld[0])
    al = bdot(mixes[4], ld[1])
    logd = -0.606531 * jax.nn.sigmoid(co[0:1] + bdot(jnp.tanh(dl), lu[0]))
    rate = jax.nn.sigmoid(co[1:2] + bdot(al, lu[1]))
    lane_a = lax.broadcasted_iota(jnp.int32, (hc, hc), 0) // HEAD
    lane_b = lax.broadcasted_iota(jnp.int32, (hc, hc), 1) // HEAD
    same = (lane_a == lane_b).astype(BF16)
    kappa = k * co[2:3]
    kappa = kappa * lax.rsqrt(head_sums(kappa * kappa, same) + 1e-05)
    t_of = lax.broadcasted_iota(jnp.int32, (LMAX, LMAX), 0)
    u_of = lax.broadcasted_iota(jnp.int32, (LMAX, LMAX), 1)
    upto = u_of <= t_of
    before = u_of < t_of
    lower = upto.astype(BF16)
    low_lane = u_of < HEAD
    side = jnp.concatenate([low_lane, low_lane], axis=0)
    levels = [((t_of >> n) == (u_of >> n) + 1) & (((t_of >> n) & 1) == 1) for n in range(7)]
    eye = (t_of == u_of).astype(F32)
    place = lax.broadcasted_iota(jnp.int32, (LMAX, hc), 0)
    chains = []
    keep = []
    for p in range(per):
        at = slice(p * LMAX, (p + 1) * LMAX)
        live = (place < lens[pl.program_id(0) * per + p]).astype(F32)
        rp, kp, vp = r[at], k[at] * live, v[at] * live
        dp = logd[at] * live
        kh = kappa[at] * live
        wr = kh * rate[at]
        d1 = dp.astype(BF16)
        d2, d3 = halves(dp - d1.astype(F32))
        cum = bdot(lower, d1) + (bdot(lower, d2) + bdot(lower, d3))
        last = cum[LMAX - 1 : LMAX]
        mid = 0.5 * last
        grow = jnp.exp(mid - cum)
        tail = jnp.exp(last - mid)
        pull = -kh * jnp.exp(cum - dp - mid)
        read = rp * jnp.exp(cum - mid)
        wb = wr * grow
        kb = kp * grow
        keep.append((live, head_sums(rp * kp * co[3:4], same) * vp))
        for q in range(hc // 128):
            ln = slice(q * 128, (q + 1) * 128)
            right = jnp.concatenate([wb[:, ln], kb[:, ln]], axis=0)
            left = jnp.concatenate([pull[:, ln], read[:, ln]], axis=0)
            pair = []
            for h in range(2):
                g = bdot(jnp.where(side == (h == 0), left, 0.0), right, 1, 1)
                pair.append(
                    (
                        jnp.where(before, g[:LMAX, :LMAX], 0.0),
                        jnp.where(before, g[:LMAX, LMAX:], 0.0),
                        jnp.where(upto, g[LMAX:, :LMAX], 0.0),
                        jnp.where(upto, g[LMAX:, LMAX:], 0.0),
                    )
                )
            chains.append((p, q, pair, vp[:, ln], wb[:, ln] * tail[:, ln], kb[:, ln] * tail[:, ln]))
    strict = [c[2][h][0] for c in chains for h in range(2)]
    inverse = [eye + jnp.where(levels[0], a, 0.0) for a in strict]
    for n in range(1, 7):
        inner = [dot3(jnp.where(levels[n], a, 0.0), t) for a, t in zip(strict, inverse)]
        inverse = [t + dot3(t, m) for t, m in zip(inverse, inner)]
    outs = {}
    for i, (p, q, pair, vq, wt, kt) in enumerate(chains):
        us, ys = [], []
        for h in range(2):
            _, b, rw, rk = pair[h]
            u = dot3(inverse[2 * i + h], bdot(b, vq))
            us.append(u)
            ys.append(bdot(jnp.concatenate([rw, rk], axis=1), jnp.concatenate([u, vq], axis=0)))
        u = jnp.where(low_lane, us[0], us[1])
        outs[p, q] = jnp.where(low_lane, ys[0], ys[1])
        final = bdot(jnp.concatenate([u, vq], axis=0), jnp.concatenate([wt, kt], axis=0), 0, 0)
        state_ref[p, 2 * q] = final[:HEAD, :HEAD].astype(BF16)
        state_ref[p, 2 * q + 1] = final[HEAD:, HEAD:].astype(BF16)
    atts = []
    for p in range(per):
        live, extra = keep[p]
        y = jnp.concatenate([outs[p, q] for q in range(hc // 128)], axis=1)
        y = (y + extra) * live
        y = y - head_sums(y, same) / HEAD
        spread = head_sums(y * y, same) / HEAD
        atts.append((y * lax.rsqrt(spread + 0.00064) * co[4:5] + co[5:6]).astype(BF16))
    out_ref[...] = bdot(jnp.concatenate(atts, axis=0), wo[...], 1, 1).astype(BF16)


def time_mix(lens, xg, gb, shift, w, ld, lu, co, wo, per):
    nb = len(xg)
    tokens, fw = xg[0].shape
    prompts = tokens // LMAX
    hc = w.shape[2]

    def full(a):
        return pl.BlockSpec(a.shape, lambda i: (0,) * a.ndim)

    rest = (gb, shift, w, ld, lu, co, wo)
    return pl.pallas_call(
        functools.partial(time_kernel, nb, per),
        grid=(prompts // per,),
        in_specs=[pl.BlockSpec(memory_space=pltpu.SMEM)]
        + [pl.BlockSpec((per * LMAX, fw), lambda i: (i, 0))] * nb
        + [full(a) for a in rest],
        out_specs=[
            pl.BlockSpec((per * LMAX, wo.shape[0]), lambda i: (i, 0)),
            pl.BlockSpec((per, hc // HEAD, HEAD, HEAD), lambda i: (i, 0, 0, 0)),
        ],
        out_shape=[
            jax.ShapeDtypeStruct((tokens, wo.shape[0]), BF16),
            jax.ShapeDtypeStruct((prompts, hc // HEAD, HEAD, HEAD), BF16),
        ],
        scratch_shapes=[pltpu.VMEM((5, per * LMAX, nb * fw), BF16)],
        compiler_params=pltpu.CompilerParams(vmem_limit_bytes=50 * 2**20),
        cost_estimate=pl.CostEstimate(flops=40 * 10**9, bytes_accessed=2**24, transcendentals=0),
    )(lens, *xg, *rest)


def norm_of(z, gain, bias):
    width = z.shape[1]
    center = jnp.sum(z, axis=1, keepdims=True) / width
    second = jnp.sum(z * z, axis=1, keepdims=True) / width
    return ((z - center) * lax.rsqrt(second - center * center + 1e-05) * gain + bias).astype(BF16)


def next_kernel(nb, x, gate, w, out):
    z = x[...].astype(F32)
    rows = z.shape[0]
    first_row = lax.broadcasted_iota(jnp.int32, z.shape, 0) % LMAX == 0
    step = jnp.where(first_row, 0.0, pltpu.roll(z, 1, 0)) - z
    for m in range(3):
        mixed = (z + step * gate[m : m + 1]).astype(BF16)
        fw = w.shape[2]
        total = jnp.zeros((rows, w.shape[3]), F32)
        for i in range(nb):
            total += bdot(mixed[:, i * fw : (i + 1) * fw], w[i, m])
        out[m] = total.astype(BF16)


def next_products(x, gate, w):
    tokens, width = x.shape
    nb, _, fw, cols = w.shape
    return pl.pallas_call(
        functools.partial(next_kernel, nb),
        grid=(tokens // LMAX,),
        in_specs=[
            pl.BlockSpec((LMAX, width), lambda i: (i, 0)),
            pl.BlockSpec(gate.shape, lambda i: (0, 0)),
            pl.BlockSpec(w.shape, lambda i: (0, 0, 0, 0)),
        ],
        out_specs=pl.BlockSpec((3, LMAX, cols), lambda i: (0, i, 0)),
        out_shape=jax.ShapeDtypeStruct((3, tokens, cols), BF16),
        compiler_params=pltpu.CompilerParams(vmem_limit_bytes=50 * 2**20),
        cost_estimate=pl.CostEstimate(flops=6 * 10**9, bytes_accessed=2**24, transcendentals=0),
    )(x, gate, w)


def per_device(
    hidden,
    lengths,
    square_matrix_shards,
    channel_mix_shards,
    lowrank_down,
    lowrank_up,
    token_shift_weights,
    attention_coefficients,
    norm_parameters,
):
    n_row = lax.axis_size("row")
    n_col = lax.axis_size("col")
    row = lax.axis_index("row")
    col = lax.axis_index("col")
    chips = n_row // 2
    tokens, fw = hidden.shape
    width = token_shift_weights.shape[1]
    chunk = tokens // n_row
    deep = square_matrix_shards.shape[1]
    hc = width // n_row
    by_row = row ^ jnp.arange(n_row)

    def to_row(x, k):
        return lax.ppermute(x, "row", [(i, i ^ k) for i in range(n_row)])

    def chunk_of(r):
        return (r % 2) * chips + r // 2

    def row_of(n):
        return (n % chips) * 2 + n // chips

    def gather_row(x):
        mine = [x] + [to_row(x, 2 * k) for k in range(1, chips)]
        return [piece for m in mine for piece in (m, to_row(m, 1))]

    def spread_row(blocks):
        return [lax.dynamic_index_in_dim(blocks, row ^ k, 0, keepdims=False) for k in range(n_row)]

    def exchange_row(blocks):
        sent = spread_row(blocks)
        return [sent[0]] + [to_row(sent[k], k) for k in range(1, n_row)]

    def sum_row(blocks):
        other = to_row(blocks[1::2], 1)
        near = (blocks[0::2].astype(F32) + other.astype(F32)).astype(BF16)
        total = near[0].astype(F32)
        for k in range(1, chips):
            total = total + to_row(near[k], 2 * k).astype(F32)
        return total

    xg = gather_row(hidden)
    norms = lax.all_gather(norm_parameters, "row", axis=0, tiled=False)
    square_low = square_matrix_shards.astype(BF16)
    early = square_low[0:4].reshape(4, deep, n_row, hc).transpose(2, 0, 1, 3).reshape(n_row, 4 * deep, hc)
    early = jnp.concatenate(exchange_row(early), axis=0)
    early = lax.all_gather(early, "col", axis=0, tiled=True)
    early = early.reshape(n_col, n_row, 4, deep, hc)
    w_in = early[:, :, 0:3].transpose(2, 1, 0, 3, 4).reshape(3, width, hc)
    w_out = jnp.take(early[:, :, 3], by_row, axis=1).transpose(1, 0, 2, 3).reshape(width, hc)
    ff = channel_mix_shards.shape[2] // n_row
    late = channel_mix_shards.astype(BF16).reshape(2, deep, n_row, ff).transpose(2, 0, 1, 3)
    late = jnp.stack(exchange_row(late))
    late = jnp.take(late, by_row, axis=0).reshape(n_row * 2 * deep, ff)
    late = lax.all_gather(late, "col", axis=0, tiled=True).reshape(n_col, n_row, 2, deep, ff)
    late = late.transpose(2, 1, 0, 3, 4).reshape(2, width, ff)
    cols = width // n_col
    last = square_low[4:7].reshape(3, deep, n_col, cols).transpose(2, 0, 1, 3)
    sent = [lax.dynamic_index_in_dim(last, col ^ k, 0, keepdims=False) for k in range(n_col)]
    got = [sent[0]] + [
        lax.ppermute(sent[k], "col", [(i, i ^ k) for i in range(n_col)]) for k in range(1, n_col)
    ]
    last = jnp.take(jnp.stack(got), col ^ jnp.arange(n_col), axis=0)
    last = last.transpose(1, 0, 2, 3).reshape(3 * n_col * deep, cols)
    last = lax.all_gather(last, "row", axis=0, tiled=True).reshape(n_row, 3, n_col * deep, cols)

    prompts = tokens // LMAX
    lens = lax.dynamic_slice_in_dim(lengths, col * prompts, prompts, 0)
    gb = jnp.take(norms[:, 0:2], by_row, axis=0).transpose(1, 0, 2).reshape(2 * n_row, fw)
    shift = jnp.take(token_shift_weights[0:5].reshape(5, n_row, fw), by_row, axis=1).reshape(5 * n_row, fw)
    down = jnp.take(lowrank_down.reshape(2, n_row, fw, -1), by_row, axis=1).reshape(lowrank_down.shape)
    up = lax.dynamic_slice_in_dim(lowrank_up, row * hc, hc, 2)
    co = lax.dynamic_slice_in_dim(attention_coefficients, row * hc, hc, 1)
    partial, states = time_mix(lens, xg, gb, shift, w_in, down, up, co, w_out, 2)

    half = prompts // 2
    share = n_row // n_col
    states = states.reshape(2, half, states.shape[1], HEAD, HEAD)
    moved = []
    for j in range(2):
        pairs = []
        for r in range(n_row):
            for c in range(n_col):
                h = (r % 2) ^ j
                pairs.append((r * n_col + c, (2 * c + h) * n_col + r // share))
        piece = lax.dynamic_index_in_dim(states, (row % 2) ^ j, 0, keepdims=False)
        moved.append(lax.ppermute(piece, ("row", "col"), pairs))
    moved = jnp.take(jnp.stack(moved), (row % 2) ^ jnp.arange(2), axis=0)
    final_state = moved.transpose(1, 0, 2, 3, 4).reshape(half, -1, HEAD * HEAD).astype(F32)

    here = chunk_of(row) * chunk
    parts = jnp.take(partial.reshape(n_row, chunk, width), chunk_of(by_row), axis=0)
    attn = sum_row(parts)
    own = jnp.stack([lax.dynamic_slice_in_dim(x, here, chunk, 0) for x in xg])
    own = jnp.take(own, by_row, axis=0).transpose(1, 0, 2).reshape(chunk, width)
    mid = (own.astype(F32) + attn).astype(BF16).astype(F32)
    gains = norms.transpose(1, 0, 2).reshape(-1, width)
    second = norm_of(mid, gains[2], gains[3]).astype(F32)
    edge = jnp.zeros_like(second[:1])
    if chunk % LMAX:
        pairs = [(row_of(n), row_of(n + 1)) for n in range(n_row - 1)]
        edge = lax.ppermute(second[-1:].astype(BF16), "row", pairs).astype(F32)
        edge = jnp.where(here % LMAX == 0, 0.0, edge)
    moved_on = jnp.concatenate([edge, second[:-1]], axis=0)
    channel_in = (second + (moved_on - second) * token_shift_weights[5]).astype(BF16)
    rows_in = jnp.concatenate(gather_row(channel_in), axis=0)
    pre = jnp.dot(rows_in, late[0], preferred_element_type=F32)
    act = jnp.square(jax.nn.relu(pre)).astype(BF16)
    mlp = lax.dot_general(act, late[1], (((1,), (1,)), ((), ())), preferred_element_type=F32)
    channel_out = sum_row(mlp.astype(BF16).reshape(n_row, chunk, width))
    out_own = (mid + channel_out).astype(BF16)
    pieces = exchange_row(out_own.reshape(chunk, n_row, fw).transpose(1, 0, 2))
    out_hidden = jnp.take(jnp.stack(pieces), row ^ row_of(jnp.arange(n_row)), axis=0).reshape(tokens, fw)

    third = norm_of(out_own.astype(F32), gains[4], gains[5])
    arrived = []
    for j in range(n_col):
        pairs = []
        for r in range(n_row):
            for c in range(n_col):
                pairs.append((r * n_col + c, (2 * c + r % 2) * n_col + ((r // 2) ^ j)))
        arrived.append(lax.ppermute(third, ("row", "col"), pairs))
    third_all = jnp.take(jnp.stack(arrived), col ^ jnp.arange(n_col), axis=0).reshape(-1, width)
    next_rkv = next_products(third_all, token_shift_weights[6:9], last)
    return (out_hidden, next_rkv, final_state)


def solution(mesh):
    return jax.shard_map(
        per_device,
        mesh=mesh,
        in_specs=(
            P("col", "row"),
            P(),
            P(None, ("row", "col"), None),
            P(None, ("row", "col"), None),
            P(),
            P(),
            P(),
            P(),
            P(None, "row"),
        ),
        out_specs=(P("col", "row"), P(None, "row", "col"), P("row", "col", None)),
        check_vma=False,
    )
```

```python
import functools

import jax
import jax.numpy as jnp
from jax import lax
from jax.experimental import pallas as pl
from jax.experimental.pallas import tpu as pltpu
from jax.sharding import PartitionSpec as P

LMAX = 128
HEAD = 64
F32 = jnp.float32
BF16 = jnp.bfloat16


def bdot(a, b, ca=1, cb=0):
    return lax.dot_general(
        a.astype(BF16), b.astype(BF16), (((ca,), (cb,)), ((), ())), preferred_element_type=F32
    )


def halves(x):
    top = x.astype(BF16)
    return top, (x - top.astype(F32)).astype(BF16)


def dot3(a, b, ca=1, cb=0):
    ah, al = halves(a)
    bh, bl = halves(b)
    return bdot(ah, bh, ca, cb) + (bdot(ah, bl, ca, cb) + bdot(al, bh, ca, cb))


def head_sums(x, same):
    top, low = halves(x)
    return bdot(top, same) + bdot(low, same)


def time_kernel(nb, nc, per, place_ref, lens, *refs):
    xg = refs[:nb]
    norms, shift, ld, lu, co = refs[nb : nb + 5]
    wt = refs[nb + 5 : nb + 5 + nc]
    even, odd, own, state_ref, mixes, w, sems = refs[-7:]
    rows = per * LMAX
    fw = xg[0].shape[1]
    width = nb * fw
    hc = w.shape[-1]
    chunk = even.shape[1]
    row, col = place_ref[0], place_ref[1]

    @pl.when(pl.program_id(0) == 0)
    def _():
        copies = [
            pltpu.make_async_copy(wt[k].at[:, m], w.at[m, :, col ^ k], sems.at[m, k])
            for m in range(4)
            for k in range(nc)
        ]
        for copy in copies:
            copy.start()
        for copy in copies:
            copy.wait()

    weight = [w[m].reshape(width, hc) for m in range(4)]
    blocks = [x[...].astype(F32) for x in xg]
    total = sum(jnp.sum(b, axis=1, keepdims=True) for b in blocks)
    square = sum(jnp.sum(b * b, axis=1, keepdims=True) for b in blocks)
    center = total / width
    scale = lax.rsqrt(square / width - center * center + 1e-05)
    first_row = lax.broadcasted_iota(jnp.int32, (rows, fw), 0) % LMAX == 0
    for i in range(nb):
        at = row ^ i
        lanes = pl.ds(pl.multiple_of(at * fw, fw), fw)
        z = (xg[i][...].astype(F32) - center) * scale * norms[at, 0:1] + norms[at, 1:2]
        z = z.astype(BF16).astype(F32)
        step = jnp.where(first_row, 0.0, pltpu.roll(z, 1, 0)) - z
        for j in range(5):
            mixes[j, :, lanes] = (z + step * shift[at, j : j + 1]).astype(BF16)
    r = bdot(mixes[0], weight[0])
    k = bdot(mixes[1], weight[1])
    v = bdot(mixes[2], weight[2])
    dl = bdot(mixes[3], ld[0])
    al = bdot(mixes[4], ld[1])
    logd = -0.606531 * jax.nn.sigmoid(co[0:1] + bdot(jnp.tanh(dl), lu[0]))
    rate = jax.nn.sigmoid(co[1:2] + bdot(al, lu[1]))
    lane_a = lax.broadcasted_iota(jnp.int32, (hc, hc), 0) // HEAD
    lane_b = lax.broadcasted_iota(jnp.int32, (hc, hc), 1) // HEAD
    same = (lane_a == lane_b).astype(BF16)
    kappa = k * co[2:3]
    kappa = kappa * lax.rsqrt(head_sums(kappa * kappa, same) + 1e-05)
    t_of = lax.broadcasted_iota(jnp.int32, (LMAX, LMAX), 0)
    u_of = lax.broadcasted_iota(jnp.int32, (LMAX, LMAX), 1)
    upto = u_of <= t_of
    before = u_of < t_of
    lower = upto.astype(BF16)
    low_lane = u_of < HEAD
    side = jnp.concatenate([low_lane, low_lane], axis=0)
    levels = [((t_of >> n) == (u_of >> n) + 1) & (((t_of >> n) & 1) == 1) for n in range(7)]
    eye = (t_of == u_of).astype(F32)
    place = lax.broadcasted_iota(jnp.int32, (LMAX, hc), 0)
    chains = []
    keep = []
    for p in range(per):
        at = slice(p * LMAX, (p + 1) * LMAX)
        live = (place < lens[pl.program_id(0) * per + p]).astype(F32)
        rp, kp, vp = r[at], k[at] * live, v[at] * live
        dp = logd[at] * live
        kh = kappa[at] * live
        wr = kh * rate[at]
        d1 = dp.astype(BF16)
        d2, d3 = halves(dp - d1.astype(F32))
        cum = bdot(lower, d1) + (bdot(lower, d2) + bdot(lower, d3))
        last = cum[LMAX - 1 : LMAX]
        mid = 0.5 * last
        grow = jnp.exp(mid - cum)
        tail = jnp.exp(last - mid)
        pull = -kh * jnp.exp(cum - dp - mid)
        read = rp * jnp.exp(cum - mid)
        wb = wr * grow
        kb = kp * grow
        keep.append((live, head_sums(rp * kp * co[3:4], same) * vp))
        for q in range(hc // 128):
            ln = slice(q * 128, (q + 1) * 128)
            right = jnp.concatenate([wb[:, ln], kb[:, ln]], axis=0)
            left = jnp.concatenate([pull[:, ln], read[:, ln]], axis=0)
            pair = []
            for h in range(2):
                g = bdot(jnp.where(side == (h == 0), left, 0.0), right, 1, 1)
                pair.append(
                    (
                        jnp.where(before, g[:LMAX, :LMAX], 0.0),
                        jnp.where(before, g[:LMAX, LMAX:], 0.0),
                        jnp.where(upto, g[LMAX:, :LMAX], 0.0),
                        jnp.where(upto, g[LMAX:, LMAX:], 0.0),
                    )
                )
            chains.append((p, q, pair, vp[:, ln], wb[:, ln] * tail[:, ln], kb[:, ln] * tail[:, ln]))
    strict = [c[2][h][0] for c in chains for h in range(2)]
    inverse = [eye + jnp.where(levels[0], a, 0.0) for a in strict]
    for n in range(1, 7):
        inner = [dot3(jnp.where(levels[n], a, 0.0), t) for a, t in zip(strict, inverse)]
        inverse = [t + dot3(t, m) for t, m in zip(inverse, inner)]
    outs = {}
    for i, (p, q, pair, vq, wt, kt) in enumerate(chains):
        us, ys = [], []
        for h in range(2):
            _, b, rw, rk = pair[h]
            u = dot3(inverse[2 * i + h], bdot(b, vq))
            us.append(u)
            ys.append(bdot(jnp.concatenate([rw, rk], axis=1), jnp.concatenate([u, vq], axis=0)))
        u = jnp.where(low_lane, us[0], us[1])
        outs[p, q] = jnp.where(low_lane, ys[0], ys[1])
        final = bdot(jnp.concatenate([u, vq], axis=0), jnp.concatenate([wt, kt], axis=0), 0, 0)
        state_ref[p, 2 * q] = final[:HEAD, :HEAD].astype(BF16)
        state_ref[p, 2 * q + 1] = final[HEAD:, HEAD:].astype(BF16)
    atts = []
    for p in range(per):
        live, extra = keep[p]
        y = jnp.concatenate([outs[p, q] for q in range(hc // 128)], axis=1)
        y = (y + extra) * live
        y = y - head_sums(y, same) / HEAD
        spread = head_sums(y * y, same) / HEAD
        atts.append((y * lax.rsqrt(spread + 0.00064) * co[4:5] + co[5:6]).astype(BF16))
    partial = bdot(jnp.concatenate(atts, axis=0), weight[3], 1, 1).astype(BF16)
    pieces = rows // chunk
    for t in range(pieces):
        n = pl.program_id(0) * pieces + t
        to = row ^ ((n % (nb // 2)) * 2 + n // (nb // 2))
        here = slice(t * chunk, (t + 1) * chunk)

        @pl.when(to == 0)
        def _():
            for i in range(nb):
                own[:, pl.ds(pl.multiple_of((row ^ i) * fw, fw), fw)] = xg[i][here]

        @pl.when(to % 2 == 0)
        def _():
            even[to // 2] = partial[here]

        @pl.when(to % 2 == 1)
        def _():
            odd[to // 2] = partial[here]


def time_mix(place, lens, xg, norms, shift, ld, lu, co, wt, extra, per):
    nb, nc = len(xg), len(wt)
    tokens, fw = xg[0].shape
    prompts = tokens // LMAX
    _, _, deep, hc = wt[0].shape
    width, chunk = nb * fw, tokens // nb

    def full(a):
        return pl.BlockSpec(a.shape, lambda i: (0,) * a.ndim)

    whole = pl.BlockSpec((nb // 2, chunk, width), lambda i: (0, 0, 0))
    rest = (norms, shift, ld, lu, co)
    return pl.pallas_call(
        functools.partial(time_kernel, nb, nc, per),
        grid=(prompts // per,),
        in_specs=[pl.BlockSpec(memory_space=pltpu.SMEM)] * 2
        + [pl.BlockSpec((per * LMAX, fw), lambda i: (i, 0))] * nb
        + [full(a) for a in rest]
        + [pl.BlockSpec(memory_space=pl.ANY)] * (nc + len(extra)),
        out_specs=[
            whole,
            whole,
            pl.BlockSpec((chunk, width), lambda i: (0, 0)),
            pl.BlockSpec((per, hc // HEAD, HEAD, HEAD), lambda i: (i, 0, 0, 0)),
        ],
        out_shape=[
            jax.ShapeDtypeStruct((nb // 2, chunk, width), BF16),
            jax.ShapeDtypeStruct((nb // 2, chunk, width), BF16),
            jax.ShapeDtypeStruct((chunk, width), BF16),
            jax.ShapeDtypeStruct((prompts, hc // HEAD, HEAD, HEAD), BF16),
        ],
        scratch_shapes=[
            pltpu.VMEM((5, per * LMAX, width), BF16),
            pltpu.VMEM((4, nb, nc, deep, hc), BF16),
            pltpu.SemaphoreType.DMA((4, nc)),
        ],
        compiler_params=pltpu.CompilerParams(vmem_limit_bytes=50 * 2**20),
        cost_estimate=pl.CostEstimate(flops=40 * 10**9, bytes_accessed=2**24, transcendentals=0),
    )(place, lens, *xg, *rest, *wt, *extra)


def shifted_mix(z, weight):
    first_row = lax.broadcasted_iota(jnp.int32, z.shape, 0) % LMAX == 0
    return (z + (jnp.where(first_row, 0.0, pltpu.roll(z, 1, 0)) - z) * weight).astype(BF16)


def settle_kernel(count, *refs):
    pieces = refs[:count]
    base, gains, out, normal, blend = refs[count:]
    total = base[...].astype(F32)
    attn = pieces[0][...].astype(F32)
    for piece in pieces[1:]:
        attn = attn + piece[...].astype(F32)
    total = (total + attn).astype(BF16)
    out[...] = total
    z = total.astype(F32)
    width = z.shape[1]
    center = jnp.sum(z, axis=1, keepdims=True) / width
    second = jnp.sum(z * z, axis=1, keepdims=True) / width
    z = (z - center) * lax.rsqrt(second - center * center + 1e-05) * gains[0:1] + gains[1:2]
    z = z.astype(BF16)
    normal[...] = z
    blend[...] = shifted_mix(z.astype(F32), gains[2:3])


def settle(pieces, base, gains):
    spec = pl.BlockSpec(memory_space=pltpu.VMEM)
    return pl.pallas_call(
        functools.partial(settle_kernel, len(pieces)),
        in_specs=[spec] * (len(pieces) + 2),
        out_specs=[spec] * 3,
        out_shape=[jax.ShapeDtypeStruct(base.shape, BF16)] * 3,
        compiler_params=pltpu.CompilerParams(vmem_limit_bytes=24 * 2**20),
        cost_estimate=pl.CostEstimate(flops=10**8, bytes_accessed=2**22, transcendentals=0),
    )(*pieces, base, gains)


def mlp_kernel(nc, chunk, *refs):
    xa, xb, late = refs[:3]
    pa, pb, w, sems = refs[-4:]
    width = xa.shape[1]
    copies = [
        [pltpu.make_async_copy(late.at[c, :, m], w.at[m, :, c], sems.at[m, c]) for c in range(nc)] for m in range(2)
    ]
    for copy in copies[0] + copies[1]:
        copy.start()
    x = jnp.concatenate([xa[...], xb[...]], axis=0)
    for copy in copies[0]:
        copy.wait()
    pre = bdot(x, w[0].reshape(width, -1))
    act = jnp.square(jnp.maximum(pre, 0.0)).astype(BF16)
    for copy in copies[1]:
        copy.wait()
    out = bdot(act, w[1].reshape(width, -1), 1, 1).astype(BF16)
    pa[...] = out[:chunk]
    pb[...] = out[chunk:]


def mlp_products(xa, xb, late, extra):
    nc, nb, _, deep, ff = late.shape
    chunk = xa.shape[0]
    spec = pl.BlockSpec(memory_space=pltpu.VMEM)
    apart = pl.BlockSpec(memory_space=pl.ANY)
    return pl.pallas_call(
        functools.partial(mlp_kernel, nc, chunk),
        in_specs=[spec, spec, apart] + [apart] * len(extra),
        out_specs=[spec, spec],
        out_shape=[jax.ShapeDtypeStruct(xa.shape, BF16)] * 2,
        scratch_shapes=[pltpu.VMEM((2, nb, nc, deep, ff), BF16), pltpu.SemaphoreType.DMA((2, nc))],
        compiler_params=pltpu.CompilerParams(vmem_limit_bytes=40 * 2**20),
        cost_estimate=pl.CostEstimate(flops=4 * 10**9, bytes_accessed=2**23, transcendentals=0),
    )(xa, xb, late, *extra)


def next_kernel(nb, nc, place_ref, *refs):
    xs = refs[:nc]
    gate = refs[nc]
    given = refs[nc + 1 : nc + 1 + nb]
    out, x, w, sems = refs[-4:]
    row, col = place_ref[0], place_ref[1]
    copies = [
        pltpu.make_async_copy(given[i].at[k], w.at[:, row ^ i, col ^ k], sems.at[i, k])
        for i in range(nb)
        for k in range(nc)
    ]
    for copy in copies:
        copy.start()
    chunk, width = xs[0].shape
    for k in range(nc):
        x[pl.ds(pl.multiple_of((col ^ k) * chunk, chunk), chunk), :] = xs[k][...]
    z = x[...].astype(F32)
    mixed = [shifted_mix(z, gate[m : m + 1]) for m in range(3)]
    for copy in copies:
        copy.wait()
    for m in range(3):
        out[m] = bdot(mixed[m], w[m].reshape(width, -1)).astype(BF16)


def next_products(place, xs, gate, given):
    nb, nc = len(given), len(xs)
    chunk, width = xs[0].shape
    _, _, deep, cols = given[0].shape
    spec = pl.BlockSpec(memory_space=pltpu.VMEM)
    return pl.pallas_call(
        functools.partial(next_kernel, nb, nc),
        in_specs=[pl.BlockSpec(memory_space=pltpu.SMEM)]
        + [spec] * (nc + 1)
        + [pl.BlockSpec(memory_space=pl.ANY)] * nb,
        out_specs=spec,
        out_shape=jax.ShapeDtypeStruct((3, nc * chunk, cols), BF16),
        scratch_shapes=[
            pltpu.VMEM((nc * chunk, width), BF16),
            pltpu.VMEM((3, nb, nc, deep, cols), BF16),
            pltpu.SemaphoreType.DMA((nb, nc)),
        ],
        compiler_params=pltpu.CompilerParams(vmem_limit_bytes=50 * 2**20),
        cost_estimate=pl.CostEstimate(flops=6 * 10**9, bytes_accessed=2**24, transcendentals=0),
    )(place, *xs, gate, *given)


def per_device(
    hidden,
    lengths,
    square_matrix_shards,
    channel_mix_shards,
    lowrank_down,
    lowrank_up,
    token_shift_weights,
    attention_coefficients,
    norm_parameters,
):
    n_row = lax.axis_size("row")
    n_col = lax.axis_size("col")
    row = lax.axis_index("row")
    col = lax.axis_index("col")
    chips = n_row // 2
    tokens, fw = hidden.shape
    width = token_shift_weights.shape[1]
    chunk = tokens // n_row
    deep = square_matrix_shards.shape[1]
    hc = width // n_row
    place = jnp.stack([row, col]).astype(jnp.int32)

    def to_row(x, k):
        return lax.ppermute(x, "row", [(i, i ^ k) for i in range(n_row)])

    def to_col(x, k):
        return lax.ppermute(x, "col", [(i, i ^ k) for i in range(n_col)])

    def chunk_of(r):
        return (r % 2) * chips + r // 2

    def row_of(n):
        return (n % chips) * 2 + n // chips

    def gather_row(x):
        mine = [x] + [to_row(x, 2 * k) for k in range(1, chips)]
        return [piece for m in mine for piece in (m, to_row(m, 1))]

    xg = gather_row(hidden)
    norms = lax.all_gather(norm_parameters, "row", axis=0, tiled=False)
    square_low = square_matrix_shards.astype(BF16)
    early = square_low[0:4].reshape(4, deep, n_row, hc).transpose(2, 0, 1, 3)
    early = lax.all_to_all(early, "row", 0, 0, tiled=True)
    early = [early] + [to_col(early, k) for k in range(1, n_col)]
    ff = channel_mix_shards.shape[2] // n_row
    late = channel_mix_shards.astype(BF16).reshape(2, deep, n_row, ff).transpose(2, 0, 1, 3)
    late_row = lax.all_to_all(late.reshape(n_row, 2 * deep, ff), "row", 0, 0, tiled=True)
    late = lax.all_gather(late_row.reshape(n_row * 2 * deep, ff), "col", axis=0, tiled=True)
    late = late.reshape(n_col, n_row, 2, deep, ff)
    cols = width // n_col
    last = square_low[4:7].reshape(3, deep, n_col, cols).transpose(2, 0, 1, 3)
    sent = [lax.dynamic_index_in_dim(last, col ^ k, 0, keepdims=False) for k in range(n_col)]
    last = jnp.stack([sent[0]] + [to_col(sent[k], k) for k in range(1, n_col)])
    last = gather_row(last)

    prompts = tokens // LMAX
    lens = lax.dynamic_slice_in_dim(lengths, col * prompts, prompts, 0)
    shift = token_shift_weights.reshape(-1, n_row, fw).transpose(1, 0, 2)
    up = lax.dynamic_slice_in_dim(lowrank_up, row * hc, hc, 2)
    co = lax.dynamic_slice_in_dim(attention_coefficients, row * hc, hc, 1)
    even, odd, own, states = time_mix(
        place, lens, xg, norms, shift, lowrank_down, up, co, early, (late_row,), 2
    )

    half = prompts // 2
    share = n_row // n_col
    states = states.reshape(2, half, states.shape[1], HEAD, HEAD)
    moved = []
    for j in range(2):
        pairs = []
        for r in range(n_row):
            for c in range(n_col):
                h = (r % 2) ^ j
                pairs.append((r * n_col + c, (2 * c + h) * n_col + r // share))
        piece = lax.dynamic_index_in_dim(states, (row % 2) ^ j, 0, keepdims=False)
        moved.append(lax.ppermute(piece, ("row", "col"), pairs))
    moved = jnp.take(jnp.stack(moved), (row % 2) ^ jnp.arange(2), axis=0)
    final_state = moved.transpose(1, 0, 2, 3, 4).reshape(half, -1, HEAD * HEAD).astype(F32)

    other = to_row(odd, 1)
    near = [(even[k].astype(F32) + other[k].astype(F32)).astype(BF16) for k in range(chips)]
    pieces = [near[0]] + [to_row(near[k], 2 * k) for k in range(1, chips)]
    gains = norms.transpose(1, 0, 2).reshape(-1, width)
    mid, second, channel_in = settle(
        pieces, own, jnp.concatenate([gains[2:4], token_shift_weights[5:6]], axis=0)
    )
    if chunk % LMAX:
        pairs = [(row_of(n), row_of(n + 1)) for n in range(n_row - 1)]
        edge = lax.ppermute(second[-1:], "row", pairs).astype(F32)
        edge = jnp.where(chunk_of(row) * chunk % LMAX == 0, 0.0, edge)
        wide = second.astype(F32)
        moved_on = jnp.concatenate([edge, wide[:-1]], axis=0)
        channel_in = (wide + (moved_on - wide) * token_shift_weights[5]).astype(BF16)
    rows_in = gather_row(channel_in)
    pieces = [None] * chips
    for k in reversed(range(chips)):
        mine, theirs = mlp_products(rows_in[2 * k], rows_in[2 * k + 1], late, last if k == chips - 1 else ())
        total = (mine.astype(F32) + to_row(theirs, 1).astype(F32)).astype(BF16)
        pieces[k] = to_row(total, 2 * k) if k else total
    out_own, third, _ = settle(
        pieces, mid, jnp.concatenate([gains[4:6], token_shift_weights[5:6]], axis=0)
    )

    arrived = []
    for j in range(n_col):
        pairs = []
        for r in range(n_row):
            for c in range(n_col):
                pairs.append((r * n_col + c, (2 * c + r % 2) * n_col + ((r // 2) ^ j)))
        arrived.append(lax.ppermute(third, ("row", "col"), pairs))
    out_blocks = lax.all_to_all(out_own.reshape(chunk, n_row, fw).transpose(1, 0, 2), "row", 0, 0, tiled=True)
    out_hidden = jnp.concatenate([out_blocks[row_of(n)] for n in range(n_row)], axis=0)
    next_rkv = next_products(place, arrived, token_shift_weights[6:9], last)
    return (out_hidden, next_rkv, final_state)


def solution(mesh):
    return jax.shard_map(
        per_device,
        mesh=mesh,
        in_specs=(
            P("col", "row"),
            P(),
            P(None, ("row", "col"), None),
            P(None, ("row", "col"), None),
            P(),
            P(),
            P(),
            P(),
            P(None, "row"),
        ),
        out_specs=(P("col", "row"), P(None, "row", "col"), P("row", "col", None)),
        check_vma=False,
    )
```

```python
import functools

import jax
import jax.numpy as jnp
from jax import lax
from jax.experimental import pallas as pl
from jax.experimental.pallas import tpu as pltpu
from jax.sharding import PartitionSpec as P

LMAX = 128
HEAD = 64
F32 = jnp.float32
BF16 = jnp.bfloat16


def bdot(a, b, ca=1, cb=0):
    return lax.dot_general(
        a.astype(BF16), b.astype(BF16), (((ca,), (cb,)), ((), ())), preferred_element_type=F32
    )


def halves(x):
    top = x.astype(BF16)
    return top, (x - top.astype(F32)).astype(BF16)


def dot3(a, b, ca=1, cb=0):
    ah, al = halves(a)
    bh, bl = halves(b)
    return bdot(ah, bh, ca, cb) + (bdot(ah, bl, ca, cb) + bdot(al, bh, ca, cb))


def head_sums(x, same):
    top, low = halves(x)
    return bdot(top, same) + bdot(low, same)


def time_kernel(nc, per, place_ref, lens, xg, norms, shift, ld, lu, co, *refs):
    wt = refs[:nc]
    even, odd, own, state_ref, mixes, w, sems = refs[-7:]
    rows = per * LMAX
    nb, _, fw = xg.shape
    width = nb * fw
    hc = w.shape[-1]
    chunk = even.shape[1]
    row, col = place_ref[0], place_ref[1]

    @pl.when(pl.program_id(0) == 0)
    def _():
        copies = [
            pltpu.make_async_copy(wt[k].at[:, m], w.at[m, :, (col + nc - k) % nc], sems.at[m, k])
            for m in range(4)
            for k in range(nc)
        ]
        for copy in copies:
            copy.start()
        for copy in copies:
            copy.wait()

    weight = [w[m].reshape(width, hc) for m in range(4)]
    blocks = [xg[i].astype(F32) for i in range(nb)]
    total = sum(jnp.sum(b, axis=1, keepdims=True) for b in blocks)
    square = sum(jnp.sum(b * b, axis=1, keepdims=True) for b in blocks)
    center = total / width
    scale = lax.rsqrt(square / width - center * center + 1e-05)
    first_row = lax.broadcasted_iota(jnp.int32, (rows, fw), 0) % LMAX == 0
    for i in range(nb):
        z = (xg[i].astype(F32) - center) * scale * norms[i, 0:1] + norms[i, 1:2]
        z = z.astype(BF16).astype(F32)
        step = jnp.where(first_row, 0.0, pltpu.roll(z, 1, 0)) - z
        for j in range(5):
            mixes[j, :, i * fw : (i + 1) * fw] = (z + step * shift[i, j : j + 1]).astype(BF16)
    r = bdot(mixes[0], weight[0])
    k = bdot(mixes[1], weight[1])
    v = bdot(mixes[2], weight[2])
    dl = bdot(mixes[3], ld[0])
    al = bdot(mixes[4], ld[1])
    logd = -0.606531 * jax.nn.sigmoid(co[0:1] + bdot(jnp.tanh(dl), lu[0]))
    rate = jax.nn.sigmoid(co[1:2] + bdot(al, lu[1]))
    lane_a = lax.broadcasted_iota(jnp.int32, (hc, hc), 0) // HEAD
    lane_b = lax.broadcasted_iota(jnp.int32, (hc, hc), 1) // HEAD
    same = (lane_a == lane_b).astype(BF16)
    kappa = k * co[2:3]
    kappa = kappa * lax.rsqrt(head_sums(kappa * kappa, same) + 1e-05)
    t_of = lax.broadcasted_iota(jnp.int32, (LMAX, LMAX), 0)
    u_of = lax.broadcasted_iota(jnp.int32, (LMAX, LMAX), 1)
    upto = u_of <= t_of
    before = u_of < t_of
    lower = upto.astype(BF16)
    low_lane = u_of < HEAD
    side = jnp.concatenate([low_lane, low_lane], axis=0)
    levels = [((t_of >> n) == (u_of >> n) + 1) & (((t_of >> n) & 1) == 1) for n in range(7)]
    eye = (t_of == u_of).astype(F32)
    place = lax.broadcasted_iota(jnp.int32, (LMAX, hc), 0)
    chains = []
    keep = []
    for p in range(per):
        at = slice(p * LMAX, (p + 1) * LMAX)
        live = (place < lens[pl.program_id(0) * per + p]).astype(F32)
        rp, kp, vp = r[at], k[at] * live, v[at] * live
        dp = logd[at] * live
        kh = kappa[at] * live
        wr = kh * rate[at]
        d1 = dp.astype(BF16)
        d2, d3 = halves(dp - d1.astype(F32))
        cum = bdot(lower, d1) + (bdot(lower, d2) + bdot(lower, d3))
        last = cum[LMAX - 1 : LMAX]
        mid = 0.5 * last
        grow = jnp.exp(mid - cum)
        tail = jnp.exp(last - mid)
        pull = -kh * jnp.exp(cum - dp - mid)
        read = rp * jnp.exp(cum - mid)
        wb = wr * grow
        kb = kp * grow
        keep.append((live, head_sums(rp * kp * co[3:4], same) * vp))
        for q in range(hc // 128):
            ln = slice(q * 128, (q + 1) * 128)
            right = jnp.concatenate([wb[:, ln], kb[:, ln]], axis=0)
            left = jnp.concatenate([pull[:, ln], read[:, ln]], axis=0)
            pair = []
            for h in range(2):
                g = bdot(jnp.where(side == (h == 0), left, 0.0), right, 1, 1)
                pair.append(
                    (
                        jnp.where(before, g[:LMAX, :LMAX], 0.0),
                        jnp.where(before, g[:LMAX, LMAX:], 0.0),
                        jnp.where(upto, g[LMAX:, :LMAX], 0.0),
                        jnp.where(upto, g[LMAX:, LMAX:], 0.0),
                    )
                )
            chains.append((p, q, pair, vp[:, ln], wb[:, ln] * tail[:, ln], kb[:, ln] * tail[:, ln]))
    strict = [c[2][h][0] for c in chains for h in range(2)]
    inverse = [eye + jnp.where(levels[0], a, 0.0) for a in strict]
    for n in range(1, 7):
        inner = [dot3(jnp.where(levels[n], a, 0.0), t) for a, t in zip(strict, inverse)]
        inverse = [t + dot3(t, m) for t, m in zip(inverse, inner)]
    outs = {}
    for i, (p, q, pair, vq, wt, kt) in enumerate(chains):
        us, ys = [], []
        for h in range(2):
            _, b, rw, rk = pair[h]
            u = dot3(inverse[2 * i + h], bdot(b, vq))
            us.append(u)
            ys.append(bdot(jnp.concatenate([rw, rk], axis=1), jnp.concatenate([u, vq], axis=0)))
        u = jnp.where(low_lane, us[0], us[1])
        outs[p, q] = jnp.where(low_lane, ys[0], ys[1])
        final = bdot(jnp.concatenate([u, vq], axis=0), jnp.concatenate([wt, kt], axis=0), 0, 0)
        state_ref[p, 2 * q] = final[:HEAD, :HEAD].astype(BF16)
        state_ref[p, 2 * q + 1] = final[HEAD:, HEAD:].astype(BF16)
    atts = []
    for p in range(per):
        live, extra = keep[p]
        y = jnp.concatenate([outs[p, q] for q in range(hc // 128)], axis=1)
        y = (y + extra) * live
        y = y - head_sums(y, same) / HEAD
        spread = head_sums(y * y, same) / HEAD
        atts.append((y * lax.rsqrt(spread + 0.00064) * co[4:5] + co[5:6]).astype(BF16))
    partial = bdot(jnp.concatenate(atts, axis=0), weight[3], 1, 1).astype(BF16)
    pieces = rows // chunk
    for t in range(pieces):
        n = pl.program_id(0) * pieces + t
        to = row ^ ((n % (nb // 2)) * 2 + n // (nb // 2))
        here = slice(t * chunk, (t + 1) * chunk)

        @pl.when(to == 0)
        def _():
            for i in range(nb):
                own[:, i * fw : (i + 1) * fw] = xg[i, here]

        @pl.when(to % 2 == 0)
        def _():
            even[to // 2] = partial[here]

        @pl.when(to % 2 == 1)
        def _():
            odd[to // 2] = partial[here]


def time_mix(place, lens, xg, norms, shift, ld, lu, co, wt, extra, per):
    nb, _, fw = xg.shape
    nc = len(wt)
    _, _, deep, hc = wt[0].shape
    prompts = lens.shape[0]
    tokens = prompts * LMAX
    width, chunk = nb * fw, tokens // nb

    def full(a):
        return pl.BlockSpec(a.shape, lambda i: (0,) * a.ndim)

    whole = pl.BlockSpec((nb // 2, chunk, width), lambda i: (0, 0, 0))
    rest = (norms, shift, ld, lu, co)
    return pl.pallas_call(
        functools.partial(time_kernel, nc, per),
        grid=(prompts // per,),
        in_specs=[pl.BlockSpec(memory_space=pltpu.SMEM)] * 2
        + [pl.BlockSpec((nb, per * LMAX, fw), lambda i: (0, i, 0))]
        + [full(a) for a in rest]
        + [pl.BlockSpec(memory_space=pl.ANY)] * (nc + len(extra)),
        out_specs=[
            whole,
            whole,
            pl.BlockSpec((chunk, width), lambda i: (0, 0)),
            pl.BlockSpec((per, hc // HEAD, HEAD, HEAD), lambda i: (i, 0, 0, 0)),
        ],
        out_shape=[
            jax.ShapeDtypeStruct((nb // 2, chunk, width), BF16),
            jax.ShapeDtypeStruct((nb // 2, chunk, width), BF16),
            jax.ShapeDtypeStruct((chunk, width), BF16),
            jax.ShapeDtypeStruct((prompts, hc // HEAD, HEAD, HEAD), BF16),
        ],
        scratch_shapes=[
            pltpu.VMEM((5, per * LMAX, width), BF16),
            pltpu.VMEM((4, nb, nc, deep, hc), BF16),
            pltpu.SemaphoreType.DMA((4, nc)),
        ],
        compiler_params=pltpu.CompilerParams(vmem_limit_bytes=50 * 2**20),
        cost_estimate=pl.CostEstimate(flops=40 * 10**9, bytes_accessed=2**24, transcendentals=0),
    )(place, lens, xg, *rest, *wt, *extra)


def shifted_mix(z, weight):
    first_row = lax.broadcasted_iota(jnp.int32, z.shape, 0) % LMAX == 0
    return (z + (jnp.where(first_row, 0.0, pltpu.roll(z, 1, 0)) - z) * weight).astype(BF16)


def settle_kernel(count, groups, quarters, place_ref, *refs):
    pieces = refs[: count * groups]
    base, gains, out, normal, blend = refs[count * groups : count * groups + 5]
    sums = []
    for g in range(groups):
        total = pieces[g * count][...].astype(F32)
        for piece in pieces[g * count + 1 : (g + 1) * count]:
            total = total + piece[...].astype(F32)
        sums.append(total)
    width = base.shape[1]
    if quarters == 1:
        added = sums[0]
    else:
        share = width // quarters
        sums = jnp.concatenate(sums, axis=1)
        sums = [sums[:, i : i + share] for i in range(0, width, share)]
        held = refs[-1]
        for q in range(quarters):
            held[(place_ref[1] + quarters - q) % quarters] = sums[q]
        deep = sums[0].shape[1] // (2 * count)
        added = jnp.concatenate(
            [held[q, :, r * deep : (r + 1) * deep] for r in range(2 * count) for q in range(quarters)], axis=1
        )
    total = (base[...].astype(F32) + added).astype(BF16)
    out[...] = total
    z = total.astype(F32)
    center = jnp.sum(z, axis=1, keepdims=True) / width
    second = jnp.sum(z * z, axis=1, keepdims=True) / width
    z = (z - center) * lax.rsqrt(second - center * center + 1e-05) * gains[0:1] + gains[1:2]
    z = z.astype(BF16)
    normal[...] = z
    blend[...] = shifted_mix(z.astype(F32), gains[2:3])


def settle(place, pieces, base, gains, quarters):
    groups, count = len(pieces), len(pieces[0])
    flat = [piece for group in pieces for piece in group]
    spec = pl.BlockSpec(memory_space=pltpu.VMEM)
    held = [pltpu.VMEM((quarters, base.shape[0], base.shape[1] // quarters), F32)] if quarters > 1 else []
    return pl.pallas_call(
        functools.partial(settle_kernel, count, groups, quarters),
        in_specs=[pl.BlockSpec(memory_space=pltpu.SMEM)] + [spec] * (len(flat) + 2),
        out_specs=[spec] * 3,
        out_shape=[jax.ShapeDtypeStruct(base.shape, BF16)] * 3,
        scratch_shapes=held,
        compiler_params=pltpu.CompilerParams(vmem_limit_bytes=24 * 2**20),
        cost_estimate=pl.CostEstimate(flops=10**6, bytes_accessed=2**12, transcendentals=0),
    )(place, *flat, base, gains)


def after_kernel(*refs):
    pass


def after(x, *earlier):
    apart = pl.BlockSpec(memory_space=pl.ANY)
    return pl.pallas_call(
        after_kernel,
        in_specs=[apart] * (1 + len(earlier)),
        out_specs=apart,
        out_shape=jax.ShapeDtypeStruct(x.shape, x.dtype),
        input_output_aliases={0: 0},
    )(x, *earlier)


def key_kernel(nb, nc, place_ref, *refs):
    xs, shards = refs[:nb], refs[nb : nb + nc]
    act, x, w, sems = refs[-4:]
    col = place_ref[1]
    chunk, width = xs[0].shape
    moves = [pltpu.make_async_copy(xs[i], x.at[i], sems.at[nc + i]) for i in range(nb)]
    copies = [
        pltpu.make_async_copy(shards[k], w.at[:, (col + nc - k) % nc], sems.at[k]) for k in range(nc)
    ]
    for copy in copies + moves:
        copy.start()
    for copy in copies:
        copy.wait()
    weight = w[...].reshape(width, -1)
    for i in range(0, nb, 2):
        moves[i].wait()
        moves[i + 1].wait()
        pre = bdot(x[i : i + 2].reshape(2 * chunk, width), weight)
        act[i * chunk : (i + 2) * chunk, :] = jnp.square(jnp.maximum(pre, 0.0)).astype(BF16)


def key_products(place, xs, shards, extra):
    nb, nc = len(xs), len(shards)
    _, deep, ff = shards[0].shape
    chunk, width = xs[0].shape
    apart = pl.BlockSpec(memory_space=pl.ANY)
    return pl.pallas_call(
        functools.partial(key_kernel, nb, nc),
        in_specs=[pl.BlockSpec(memory_space=pltpu.SMEM)] + [apart] * (nb + nc + len(extra)),
        out_specs=pl.BlockSpec(memory_space=pltpu.VMEM),
        out_shape=jax.ShapeDtypeStruct((nb * chunk, ff), BF16),
        scratch_shapes=[
            pltpu.VMEM((nb, chunk, width), BF16),
            pltpu.VMEM((nb, nc, deep, ff), BF16),
            pltpu.SemaphoreType.DMA((nc + nb,)),
        ],
        compiler_params=pltpu.CompilerParams(vmem_limit_bytes=40 * 2**20),
        cost_estimate=pl.CostEstimate(flops=10**6, bytes_accessed=2**12, transcendentals=0),
    )(place, *xs, *shards, *extra)


def value_kernel(count, act, *refs):
    shards, (even, odd) = refs[:count], refs[-2:]
    nb = 2 * even.shape[0]
    chunk = even.shape[1]
    start = 0
    for q in range(count):
        weight = shards[q][...].reshape(-1, shards[q].shape[-1])
        at = slice(start, start + weight.shape[0])
        start += weight.shape[0]
        for k in range(nb // 2):
            out = bdot(act[2 * k * chunk : (2 * k + 2) * chunk, :], weight, 1, 1).astype(BF16)
            even[k, :, at] = out[:chunk]
            odd[k, :, at] = out[chunk:]


def value_products(nb, act, shards):
    deep = shards[0].shape[1]
    chunk = act.shape[0] // nb
    width = sum(x.shape[0] for x in shards) * deep

    spec = pl.BlockSpec(memory_space=pltpu.VMEM)
    return pl.pallas_call(
        functools.partial(value_kernel, len(shards)),
        in_specs=[spec] * (1 + len(shards)),
        out_specs=[spec] * 2,
        out_shape=[jax.ShapeDtypeStruct((nb // 2, chunk, width), BF16)] * 2,
        compiler_params=pltpu.CompilerParams(vmem_limit_bytes=40 * 2**20),
        cost_estimate=pl.CostEstimate(flops=10**6, bytes_accessed=2**12, transcendentals=0),
    )(act, *shards)


def next_kernel(nc, place_ref, *refs):
    xs = refs[:nc]
    gate, given = refs[nc : nc + 2]
    out, x, w, sems = refs[-4:]
    col = place_ref[1]
    copies = [
        pltpu.make_async_copy(given.at[:, k, m], w.at[m, :, col ^ k], sems.at[m, k])
        for m in range(3)
        for k in range(nc)
    ]
    for copy in copies:
        copy.start()
    chunk, width = xs[0].shape
    for k in range(nc):
        x[pl.ds(pl.multiple_of((col ^ k) * chunk, chunk), chunk), :] = xs[k][...]
    z = x[...].astype(F32)
    mixed = shifted_mix(z, gate[0:1])
    for copy in copies:
        copy.wait()
    for m in range(3):
        out[m] = bdot(mixed, w[m].reshape(width, -1)).astype(BF16)
        if m < 2:
            mixed = shifted_mix(z, gate[m + 1 : m + 2])


def next_products(place, xs, gate, given):
    nc = len(xs)
    chunk, width = xs[0].shape
    nb, _, _, deep, cols = given.shape
    spec = pl.BlockSpec(memory_space=pltpu.VMEM)
    return pl.pallas_call(
        functools.partial(next_kernel, nc),
        in_specs=[pl.BlockSpec(memory_space=pltpu.SMEM)]
        + [spec] * (nc + 1)
        + [pl.BlockSpec(memory_space=pl.ANY)],
        out_specs=spec,
        out_shape=jax.ShapeDtypeStruct((3, nc * chunk, cols), BF16),
        scratch_shapes=[
            pltpu.VMEM((nc * chunk, width), BF16),
            pltpu.VMEM((3, nb, nc, deep, cols), BF16),
            pltpu.SemaphoreType.DMA((3, nc)),
        ],
        compiler_params=pltpu.CompilerParams(vmem_limit_bytes=50 * 2**20),
        cost_estimate=pl.CostEstimate(flops=10**6, bytes_accessed=2**12, transcendentals=0),
    )(place, *xs, gate, given)


def per_device(
    hidden,
    lengths,
    square_matrix_shards,
    channel_mix_shards,
    lowrank_down,
    lowrank_up,
    token_shift_weights,
    attention_coefficients,
    norm_parameters,
):
    n_row = lax.axis_size("row")
    n_col = lax.axis_size("col")
    row = lax.axis_index("row")
    col = lax.axis_index("col")
    chips = n_row // 2
    tokens, fw = hidden.shape
    width = token_shift_weights.shape[1]
    chunk = tokens // n_row
    deep = square_matrix_shards.shape[1]
    hc = width // n_row
    place = jnp.stack([row, col]).astype(jnp.int32)

    def to_row(x, k):
        return lax.ppermute(x, "row", [(i, i ^ k) for i in range(n_row)])

    def to_col(x, k):
        return lax.ppermute(x, "col", [(i, i ^ k) for i in range(n_col)])

    def chunk_of(r):
        return (r % 2) * chips + r // 2

    def row_of(n):
        return (n % chips) * 2 + n // chips

    def gather_row(x):
        mine = [x] + [to_row(x, 2 * k) for k in range(1, chips)]
        return [piece for m in mine for piece in (m, to_row(m, 1))]

    def ring(x):
        return lax.ppermute(x, "col", [(i, (i + 1) % n_col) for i in range(n_col)])

    def relay(x):
        return lax.all_to_all(x, "row", 0, 0, tiled=True)

    moving = square_matrix_shards[0:4].astype(BF16).reshape(4, deep, n_row, hc).transpose(2, 0, 1, 3)
    early = [relay(moving)]
    cols = width // n_col
    sent = [
        lax.dynamic_slice_in_dim(square_matrix_shards[4:7], (col ^ k) * cols, cols, 2).astype(BF16)
        for k in range(n_col)
    ]
    last = jnp.stack([sent[0]] + [to_col(sent[k], k) for k in range(1, n_col)])
    early[0] = after(early[0], last)
    for k in range(1, n_col):
        early.append(ring(early[-1]))
    top = lax.reduce_precision(norm_parameters, 8, 7)
    middle = lax.reduce_precision(norm_parameters - top, 8, 7)
    terms = jnp.concatenate([top, middle, norm_parameters - top - middle], axis=0).astype(BF16)
    terms = jnp.pad(terms, ((0, -terms.shape[0] % 16), (0, 0)))
    xg = lax.all_gather(after(jnp.concatenate([hidden, terms], axis=0), early[0]), "row", axis=0, tiled=True)
    xg = xg.reshape(n_row, -1, fw)
    count = norm_parameters.shape[0]
    norms = xg[:, tokens : tokens + 3 * count].astype(F32)
    norms = norms[:, :count] + norms[:, count : 2 * count] + norms[:, 2 * count :]
    last = last.reshape(n_col * 3 * deep, cols)
    last = lax.all_gather(last, "row", axis=0, tiled=True).reshape(n_row, n_col, 3, deep, cols)
    ff = channel_mix_shards.shape[2] // n_row
    late = channel_mix_shards.astype(BF16).reshape(2, deep, n_row, ff).transpose(2, 0, 1, 3)
    late = relay(after(late, early[0]))
    keys = [after(late[:, 0], early[-1])]
    values = [after(late[:, 1], early[-1])]
    keys.append(ring(keys[0]))
    values.append(ring(values[0]))

    prompts = tokens // LMAX
    lens = lax.dynamic_slice_in_dim(lengths, col * prompts, prompts, 0)
    shift = token_shift_weights.reshape(-1, n_row, fw).transpose(1, 0, 2)
    up = lax.dynamic_slice_in_dim(lowrank_up, row * hc, hc, 2)
    co = lax.dynamic_slice_in_dim(attention_coefficients, row * hc, hc, 1)
    even, odd, own, states = time_mix(
        place, lens, xg, norms, shift, lowrank_down, up, co, early, (keys[0], values[0]), 2
    )

    keys[1], values[1] = after(keys[1], odd), after(values[1], odd)
    for k in range(2, n_col - 1):
        keys.append(ring(keys[-1]))
        values.append(ring(values[-1]))
    other = to_row(after(odd, keys[1], values[1]), 1)
    near = [(even[k].astype(F32) + other[k].astype(F32)).astype(BF16) for k in range(chips)]
    pieces = [near[0]] + [to_row(near[k], 2 * k) for k in range(1, chips)]
    gains = norms.transpose(1, 0, 2).reshape(-1, width)
    mid, second, channel_in = settle(
        place, [pieces], own, jnp.concatenate([gains[2:4], token_shift_weights[5:6]], axis=0), 1
    )
    if chunk % LMAX:
        pairs = [(row_of(n), row_of(n + 1)) for n in range(n_row - 1)]
        edge = lax.ppermute(second[-1:], "row", pairs).astype(F32)
        edge = jnp.where(chunk_of(row) * chunk % LMAX == 0, 0.0, edge)
        wide = second.astype(F32)
        moved_on = jnp.concatenate([edge, wide[:-1]], axis=0)
        channel_in = (wide + (moved_on - wide) * token_shift_weights[5]).astype(BF16)
    keys[-1], values[-1] = after(keys[-1], mid), after(values[-1], mid)
    keys.append(ring(keys[-1]))
    values.append(ring(values[-1]))
    rows_in = [channel_in] + [to_row(channel_in, 2 * k) for k in range(1, chips)]
    rows_in = [piece for x in rows_in for piece in (x, to_row(x, 1))]
    act = key_products(place, rows_in, keys, (last,))
    pieces = []
    for group in (values[:-1], values[-1:]):
        even, odd = value_products(n_row, act, group)
        other = to_row(odd, 1)
        near = [(even[k].astype(F32) + other[k].astype(F32)).astype(BF16) for k in range(chips)]
        pieces.append([near[0]] + [to_row(near[k], 2 * k) for k in range(1, chips)])
    out_own, third, _ = settle(
        place, pieces, mid, jnp.concatenate([gains[4:6], token_shift_weights[5:6]], axis=0), n_col
    )
    half = prompts // 2
    share = n_row // n_col
    states = after(states, out_own).reshape(2, half, states.shape[1], HEAD, HEAD)
    moved = []
    for j in range(2):
        pairs = []
        for r in range(n_row):
            for c in range(n_col):
                h = (r % 2) ^ j
                pairs.append((r * n_col + c, (2 * c + h) * n_col + r // share))
        piece = lax.dynamic_index_in_dim(states, (row % 2) ^ j, 0, keepdims=False)
        moved.append(lax.ppermute(piece, ("row", "col"), pairs))
    settled = jnp.take(jnp.stack(moved), (row % 2) ^ jnp.arange(2), axis=0)
    final_state = settled.transpose(1, 0, 2, 3, 4).reshape(half, -1, HEAD * HEAD).astype(F32)

    arrived = []
    for j in range(n_col):
        pairs = []
        for r in range(n_row):
            for c in range(n_col):
                pairs.append((r * n_col + c, (2 * c + r % 2) * n_col + ((r // 2) ^ j)))
        arrived.append(lax.ppermute(third, ("row", "col"), pairs))
    blocks = relay(out_own.reshape(chunk, n_row, fw).transpose(1, 0, 2))
    out_hidden = blocks.reshape(chips, 2, chunk, fw).transpose(1, 0, 2, 3).reshape(tokens, fw)
    next_rkv = next_products(place, arrived, token_shift_weights[6:9], last)
    return (out_hidden, next_rkv, final_state)


def solution(mesh):
    return jax.shard_map(
        per_device,
        mesh=mesh,
        in_specs=(
            P("col", "row"),
            P(),
            P(None, ("row", "col"), None),
            P(None, ("row", "col"), None),
            P(),
            P(),
            P(),
            P(),
            P(None, "row"),
        ),
        out_specs=(P("col", "row"), P(None, "row", "col"), P("row", "col", None)),
        check_vma=False,
    )
```

```python
import functools

import jax
import jax.numpy as jnp
from jax import lax
from jax.experimental import pallas as pl
from jax.experimental.pallas import tpu as pltpu
from jax.sharding import PartitionSpec as P

LMAX = 128
HEAD = 64
F32 = jnp.float32
BF16 = jnp.bfloat16


def bdot(a, b, ca=1, cb=0):
    return lax.dot_general(
        a.astype(BF16), b.astype(BF16), (((ca,), (cb,)), ((), ())), preferred_element_type=F32
    )


def halves(x):
    top = x.astype(BF16)
    return top, (x - top.astype(F32)).astype(BF16)


def dot3(a, b, ca=1, cb=0):
    ah, al = halves(a)
    bh, bl = halves(b)
    return bdot(ah, bh, ca, cb) + (bdot(ah, bl, ca, cb) + bdot(al, bh, ca, cb))


def head_sums(x, same):
    top, low = halves(x)
    return bdot(top, same) + bdot(low, same)


def time_kernel(nc, per, place_ref, lens, xg, norms, shift, ld, lu, co, *refs):
    wt = refs[:nc]
    even, odd, own, state_ref, mixes, w, sems = refs[-7:]
    rows = per * LMAX
    nb, _, fw = xg.shape
    width = nb * fw
    hc = w.shape[-1]
    chunk = even.shape[1]
    row, col = place_ref[0], place_ref[1]

    @pl.when(pl.program_id(0) == 0)
    def _():
        copies = [
            pltpu.make_async_copy(wt[k].at[:, m], w.at[m, :, (col + nc - k) % nc], sems.at[m, k])
            for m in range(4)
            for k in range(nc)
        ]
        for copy in copies:
            copy.start()
        for copy in copies:
            copy.wait()

    weight = [w[m].reshape(width, hc) for m in range(4)]
    blocks = [xg[i].astype(F32) for i in range(nb)]
    total = sum(jnp.sum(b, axis=1, keepdims=True) for b in blocks)
    square = sum(jnp.sum(b * b, axis=1, keepdims=True) for b in blocks)
    center = total / width
    scale = lax.rsqrt(square / width - center * center + 1e-05)
    first_row = lax.broadcasted_iota(jnp.int32, (rows, fw), 0) % LMAX == 0
    for i in range(nb):
        z = (xg[i].astype(F32) - center) * scale * norms[i, 0:1] + norms[i, 1:2]
        z = z.astype(BF16).astype(F32)
        step = jnp.where(first_row, 0.0, pltpu.roll(z, 1, 0)) - z
        for j in range(5):
            mixes[j, :, i * fw : (i + 1) * fw] = (z + step * shift[i, j : j + 1]).astype(BF16)
    r = bdot(mixes[0], weight[0])
    k = bdot(mixes[1], weight[1])
    v = bdot(mixes[2], weight[2])
    dl = bdot(mixes[3], ld[0])
    al = bdot(mixes[4], ld[1])
    logd = -0.606531 * jax.nn.sigmoid(co[0:1] + bdot(jnp.tanh(dl), lu[0]))
    rate = jax.nn.sigmoid(co[1:2] + bdot(al, lu[1]))
    lane_a = lax.broadcasted_iota(jnp.int32, (hc, hc), 0) // HEAD
    lane_b = lax.broadcasted_iota(jnp.int32, (hc, hc), 1) // HEAD
    same = (lane_a == lane_b).astype(BF16)
    kappa = k * co[2:3]
    kappa = kappa * lax.rsqrt(head_sums(kappa * kappa, same) + 1e-05)
    t_of = lax.broadcasted_iota(jnp.int32, (LMAX, LMAX), 0)
    u_of = lax.broadcasted_iota(jnp.int32, (LMAX, LMAX), 1)
    upto = u_of <= t_of
    before = u_of < t_of
    lower = upto.astype(BF16)
    low_lane = u_of < HEAD
    side = jnp.concatenate([low_lane, low_lane], axis=0)
    levels = [((t_of >> n) == (u_of >> n) + 1) & (((t_of >> n) & 1) == 1) for n in range(7)]
    eye = (t_of == u_of).astype(F32)
    place = lax.broadcasted_iota(jnp.int32, (LMAX, hc), 0)
    chains = []
    keep = []
    for p in range(per):
        at = slice(p * LMAX, (p + 1) * LMAX)
        live = (place < lens[pl.program_id(0) * per + p]).astype(F32)
        rp, kp, vp = r[at], k[at] * live, v[at] * live
        dp = logd[at] * live
        kh = kappa[at] * live
        wr = kh * rate[at]
        d1 = dp.astype(BF16)
        d2, d3 = halves(dp - d1.astype(F32))
        cum = bdot(lower, d1) + (bdot(lower, d2) + bdot(lower, d3))
        last = cum[LMAX - 1 : LMAX]
        mid = 0.5 * last
        grow = jnp.exp(mid - cum)
        tail = jnp.exp(last - mid)
        pull = -kh * jnp.exp(cum - dp - mid)
        read = rp * jnp.exp(cum - mid)
        wb = wr * grow
        kb = kp * grow
        keep.append((live, head_sums(rp * kp * co[3:4], same) * vp))
        for q in range(hc // 128):
            ln = slice(q * 128, (q + 1) * 128)
            right = jnp.concatenate([wb[:, ln], kb[:, ln]], axis=0)
            left = jnp.concatenate([pull[:, ln], read[:, ln]], axis=0)
            pair = []
            for h in range(2):
                g = bdot(jnp.where(side == (h == 0), left, 0.0), right, 1, 1)
                pair.append(
                    (
                        jnp.where(before, g[:LMAX, :LMAX], 0.0),
                        jnp.where(before, g[:LMAX, LMAX:], 0.0),
                        jnp.where(upto, g[LMAX:, :LMAX], 0.0),
                        jnp.where(upto, g[LMAX:, LMAX:], 0.0),
                    )
                )
            chains.append((p, q, pair, vp[:, ln], wb[:, ln] * tail[:, ln], kb[:, ln] * tail[:, ln]))
    strict = [c[2][h][0] for c in chains for h in range(2)]
    inverse = [eye + jnp.where(levels[0], a, 0.0) for a in strict]
    for n in range(1, 7):
        inner = [dot3(jnp.where(levels[n], a, 0.0), t) for a, t in zip(strict, inverse)]
        inverse = [t + dot3(t, m) for t, m in zip(inverse, inner)]
    outs = {}
    for i, (p, q, pair, vq, wt, kt) in enumerate(chains):
        us, ys = [], []
        for h in range(2):
            _, b, rw, rk = pair[h]
            u = dot3(inverse[2 * i + h], bdot(b, vq))
            us.append(u)
            ys.append(bdot(jnp.concatenate([rw, rk], axis=1), jnp.concatenate([u, vq], axis=0)))
        u = jnp.where(low_lane, us[0], us[1])
        outs[p, q] = jnp.where(low_lane, ys[0], ys[1])
        final = bdot(jnp.concatenate([u, vq], axis=0), jnp.concatenate([wt, kt], axis=0), 0, 0)
        state_ref[p, 2 * q] = final[:HEAD, :HEAD].astype(BF16)
        state_ref[p, 2 * q + 1] = final[HEAD:, HEAD:].astype(BF16)
    atts = []
    for p in range(per):
        live, extra = keep[p]
        y = jnp.concatenate([outs[p, q] for q in range(hc // 128)], axis=1)
        y = (y + extra) * live
        y = y - head_sums(y, same) / HEAD
        spread = head_sums(y * y, same) / HEAD
        atts.append((y * lax.rsqrt(spread + 0.00064) * co[4:5] + co[5:6]).astype(BF16))
    partial = bdot(jnp.concatenate(atts, axis=0), weight[3], 1, 1).astype(BF16)
    pieces = rows // chunk
    for t in range(pieces):
        n = pl.program_id(0) * pieces + t
        to = row ^ ((n % (nb // 2)) * 2 + n // (nb // 2))
        here = slice(t * chunk, (t + 1) * chunk)

        @pl.when(to == 0)
        def _():
            for i in range(nb):
                own[:, i * fw : (i + 1) * fw] = xg[i, here]

        @pl.when(to % 2 == 0)
        def _():
            even[to // 2] = partial[here]

        @pl.when(to % 2 == 1)
        def _():
            odd[to // 2] = partial[here]


def time_mix(place, lens, xg, norms, shift, ld, lu, co, wt, extra, per):
    nb, _, fw = xg.shape
    nc = len(wt)
    _, _, deep, hc = wt[0].shape
    prompts = lens.shape[0]
    tokens = prompts * LMAX
    width, chunk = nb * fw, tokens // nb

    def full(a):
        return pl.BlockSpec(a.shape, lambda i: (0,) * a.ndim)

    whole = pl.BlockSpec((nb // 2, chunk, width), lambda i: (0, 0, 0))
    rest = (norms, shift, ld, lu, co)
    return pl.pallas_call(
        functools.partial(time_kernel, nc, per),
        grid=(prompts // per,),
        in_specs=[pl.BlockSpec(memory_space=pltpu.SMEM)] * 2
        + [pl.BlockSpec((nb, per * LMAX, fw), lambda i: (0, i, 0))]
        + [full(a) for a in rest]
        + [pl.BlockSpec(memory_space=pl.ANY)] * (nc + len(extra)),
        out_specs=[
            whole,
            whole,
            pl.BlockSpec((chunk, width), lambda i: (0, 0)),
            pl.BlockSpec((per, hc // HEAD, HEAD, HEAD), lambda i: (i, 0, 0, 0)),
        ],
        out_shape=[
            jax.ShapeDtypeStruct((nb // 2, chunk, width), BF16),
            jax.ShapeDtypeStruct((nb // 2, chunk, width), BF16),
            jax.ShapeDtypeStruct((chunk, width), BF16),
            jax.ShapeDtypeStruct((prompts, hc // HEAD, HEAD, HEAD), BF16),
        ],
        scratch_shapes=[
            pltpu.VMEM((5, per * LMAX, width), BF16),
            pltpu.VMEM((4, nb, nc, deep, hc), BF16),
            pltpu.SemaphoreType.DMA((4, nc)),
        ],
        compiler_params=pltpu.CompilerParams(vmem_limit_bytes=50 * 2**20),
        cost_estimate=pl.CostEstimate(flops=40 * 10**9, bytes_accessed=2**24, transcendentals=0),
    )(place, lens, xg, *rest, *wt, *extra)


def shifted_mix(z, weight):
    first_row = lax.broadcasted_iota(jnp.int32, z.shape, 0) % LMAX == 0
    return (z + (jnp.where(first_row, 0.0, pltpu.roll(z, 1, 0)) - z) * weight).astype(BF16)


def settle_kernel(count, groups, quarters, place_ref, *refs):
    pieces = refs[: count * groups]
    base, gains, out, normal, blend = refs[count * groups : count * groups + 5]
    sums = []
    for g in range(groups):
        total = pieces[g * count][...].astype(F32)
        for piece in pieces[g * count + 1 : (g + 1) * count]:
            total = total + piece[...].astype(F32)
        sums.append(total)
    width = base.shape[1]
    if quarters == 1:
        added = sums[0]
    else:
        share = width // quarters
        sums = jnp.concatenate(sums, axis=1)
        sums = [sums[:, i : i + share] for i in range(0, width, share)]
        held = refs[-1]
        order = list(range(quarters - 2)) + [quarters - 1, quarters - 2]
        for q in range(quarters):
            held[(place_ref[1] + quarters - order[q]) % quarters] = sums[q]
        deep = sums[0].shape[1] // (2 * count)
        added = jnp.concatenate(
            [held[q, :, r * deep : (r + 1) * deep] for r in range(2 * count) for q in range(quarters)], axis=1
        )
    total = (base[...].astype(F32) + added).astype(BF16)
    out[...] = total
    z = total.astype(F32)
    center = jnp.sum(z, axis=1, keepdims=True) / width
    second = jnp.sum(z * z, axis=1, keepdims=True) / width
    z = (z - center) * lax.rsqrt(second - center * center + 1e-05) * gains[0:1] + gains[1:2]
    z = z.astype(BF16)
    normal[...] = z
    blend[...] = shifted_mix(z.astype(F32), gains[2:3])


def settle(place, pieces, base, gains, quarters):
    groups, count = len(pieces), len(pieces[0])
    flat = [piece for group in pieces for piece in group]
    spec = pl.BlockSpec(memory_space=pltpu.VMEM)
    held = [pltpu.VMEM((quarters, base.shape[0], base.shape[1] // quarters), F32)] if quarters > 1 else []
    return pl.pallas_call(
        functools.partial(settle_kernel, count, groups, quarters),
        in_specs=[pl.BlockSpec(memory_space=pltpu.SMEM)] + [spec] * (len(flat) + 2),
        out_specs=[spec] * 3,
        out_shape=[jax.ShapeDtypeStruct(base.shape, BF16)] * 3,
        scratch_shapes=held,
        compiler_params=pltpu.CompilerParams(vmem_limit_bytes=24 * 2**20),
        cost_estimate=pl.CostEstimate(flops=10**6, bytes_accessed=2**12, transcendentals=0),
    )(place, *flat, base, gains)


def after_kernel(*refs):
    pass


def after(x, *earlier):
    apart = pl.BlockSpec(memory_space=pl.ANY)
    return pl.pallas_call(
        after_kernel,
        in_specs=[apart] * (1 + len(earlier)),
        out_specs=apart,
        out_shape=jax.ShapeDtypeStruct(x.shape, x.dtype),
        input_output_aliases={0: 0},
    )(x, *earlier)


def key_kernel(nb, nc, place_ref, *refs):
    xs, shards = refs[:nb], refs[nb : nb + nc]
    act, x, w, sems = refs[-4:]
    col = place_ref[1]
    chunk, width = xs[0].shape
    moves = [pltpu.make_async_copy(xs[i], x.at[i], sems.at[nc + i]) for i in range(nb)]
    copies = [
        pltpu.make_async_copy(shards[k], w.at[:, (col + nc - k) % nc], sems.at[k]) for k in range(nc)
    ]
    for copy in copies + moves:
        copy.start()
    for copy in copies:
        copy.wait()
    weight = w[...].reshape(width, -1)
    for i in range(0, nb, 2):
        moves[i].wait()
        moves[i + 1].wait()
        pre = bdot(x[i : i + 2].reshape(2 * chunk, width), weight)
        act[i * chunk : (i + 2) * chunk, :] = jnp.square(jnp.maximum(pre, 0.0)).astype(BF16)


def key_products(place, xs, shards, extra):
    nb, nc = len(xs), len(shards)
    _, deep, ff = shards[0].shape
    chunk, width = xs[0].shape
    apart = pl.BlockSpec(memory_space=pl.ANY)
    return pl.pallas_call(
        functools.partial(key_kernel, nb, nc),
        in_specs=[pl.BlockSpec(memory_space=pltpu.SMEM)] + [apart] * (nb + nc + len(extra)),
        out_specs=pl.BlockSpec(memory_space=pltpu.VMEM),
        out_shape=jax.ShapeDtypeStruct((nb * chunk, ff), BF16),
        scratch_shapes=[
            pltpu.VMEM((nb, chunk, width), BF16),
            pltpu.VMEM((nb, nc, deep, ff), BF16),
            pltpu.SemaphoreType.DMA((nc + nb,)),
        ],
        compiler_params=pltpu.CompilerParams(vmem_limit_bytes=40 * 2**20),
        cost_estimate=pl.CostEstimate(flops=10**6, bytes_accessed=2**12, transcendentals=0),
    )(place, *xs, *shards, *extra)


def value_kernel(count, act, *refs):
    shards, (even, low, high) = refs[:count], refs[-3:]
    chips, chunk, _ = even.shape
    start = 0
    for q in range(count):
        weight = shards[q][...].reshape(-1, shards[q].shape[-1])
        at = slice(start, start + weight.shape[0])
        start += weight.shape[0]
        for k in range(chips):
            out = bdot(act[2 * k * chunk : (2 * k + 2) * chunk, :], weight, 1, 1).astype(BF16)
            even[k, :, at] = out[:chunk]
            odd = low if k < chips // 2 else high
            odd[k % (chips // 2), :, at] = out[chunk:]


def value_products(nb, act, shards, extra):
    deep = shards[0].shape[1]
    chunk = act.shape[0] // nb
    width = sum(x.shape[0] for x in shards) * deep
    spec = pl.BlockSpec(memory_space=pltpu.VMEM)
    return pl.pallas_call(
        functools.partial(value_kernel, len(shards)),
        in_specs=[spec] * (1 + len(shards)) + [pl.BlockSpec(memory_space=pl.ANY)] * len(extra),
        out_specs=[spec] * 3,
        out_shape=[jax.ShapeDtypeStruct((n, chunk, width), BF16) for n in (nb // 2, nb // 4, nb // 4)],
        compiler_params=pltpu.CompilerParams(vmem_limit_bytes=40 * 2**20),
        cost_estimate=pl.CostEstimate(flops=10**6, bytes_accessed=2**12, transcendentals=0),
    )(act, *shards, *extra)


def next_kernel(nc, place_ref, *refs):
    xs = refs[:nc]
    gate, given = refs[nc : nc + 2]
    out, x, w, sems = refs[-4:]
    col = place_ref[1]
    copies = [
        pltpu.make_async_copy(given.at[:, k, m], w.at[m, :, col ^ k], sems.at[m, k])
        for m in range(3)
        for k in range(nc)
    ]
    for copy in copies:
        copy.start()
    chunk, width = xs[0].shape
    for k in range(nc):
        at = col ^ k ^ (place_ref[0] % 2 * (nc // 2))
        x[pl.ds(pl.multiple_of(at * chunk, chunk), chunk), :] = xs[k][...]
    z = x[...].astype(F32)
    mixed = shifted_mix(z, gate[0:1])
    for copy in copies:
        copy.wait()
    for m in range(3):
        out[m] = bdot(mixed, w[m].reshape(width, -1)).astype(BF16)
        if m < 2:
            mixed = shifted_mix(z, gate[m + 1 : m + 2])


def next_products(place, xs, gate, given):
    nc = len(xs)
    chunk, width = xs[0].shape
    nb, _, _, deep, cols = given.shape
    spec = pl.BlockSpec(memory_space=pltpu.VMEM)
    return pl.pallas_call(
        functools.partial(next_kernel, nc),
        in_specs=[pl.BlockSpec(memory_space=pltpu.SMEM)]
        + [spec] * (nc + 1)
        + [pl.BlockSpec(memory_space=pl.ANY)],
        out_specs=spec,
        out_shape=jax.ShapeDtypeStruct((3, nc * chunk, cols), BF16),
        scratch_shapes=[
            pltpu.VMEM((nc * chunk, width), BF16),
            pltpu.VMEM((3, nb, nc, deep, cols), BF16),
            pltpu.SemaphoreType.DMA((3, nc)),
        ],
        compiler_params=pltpu.CompilerParams(vmem_limit_bytes=50 * 2**20),
        cost_estimate=pl.CostEstimate(flops=10**6, bytes_accessed=2**12, transcendentals=0),
    )(place, *xs, gate, given)


def per_device(
    hidden,
    lengths,
    square_matrix_shards,
    channel_mix_shards,
    lowrank_down,
    lowrank_up,
    token_shift_weights,
    attention_coefficients,
    norm_parameters,
):
    n_row = lax.axis_size("row")
    n_col = lax.axis_size("col")
    row = lax.axis_index("row")
    col = lax.axis_index("col")
    chips = n_row // 2
    tokens, fw = hidden.shape
    width = token_shift_weights.shape[1]
    chunk = tokens // n_row
    deep = square_matrix_shards.shape[1]
    hc = width // n_row
    place = jnp.stack([row, col]).astype(jnp.int32)

    def to_row(x, k):
        return lax.ppermute(x, "row", [(i, i ^ k) for i in range(n_row)])

    def to_col(x, k):
        return lax.ppermute(x, "col", [(i, i ^ k) for i in range(n_col)])

    def chunk_of(r):
        return (r % 2) * chips + r // 2

    def row_of(n):
        return (n % chips) * 2 + n // chips

    def gather_row(x):
        mine = [x] + [to_row(x, 2 * k) for k in range(1, chips)]
        return [piece for m in mine for piece in (m, to_row(m, 1))]

    def ring(x):
        return lax.ppermute(x, "col", [(i, (i + 1) % n_col) for i in range(n_col)])

    def back(x):
        return lax.ppermute(x, "col", [(i, (i - 1) % n_col) for i in range(n_col)])

    def relay(x):
        return lax.all_to_all(x, "row", 0, 0, tiled=True)

    moving = square_matrix_shards[0:4].astype(BF16).reshape(4, deep, n_row, hc).transpose(2, 0, 1, 3)
    early = [relay(moving)]
    cols = width // n_col
    sent = [
        lax.dynamic_slice_in_dim(square_matrix_shards[4:7], (col ^ k) * cols, cols, 2).astype(BF16)
        for k in range(n_col)
    ]
    last = jnp.stack([sent[0]] + [to_col(sent[k], k) for k in range(1, n_col)])
    early[0] = after(early[0], last)
    for k in range(1, n_col):
        early.append(ring(early[-1]))
    top = lax.reduce_precision(norm_parameters, 8, 7)
    middle = lax.reduce_precision(norm_parameters - top, 8, 7)
    terms = jnp.concatenate([top, middle, norm_parameters - top - middle], axis=0).astype(BF16)
    terms = jnp.pad(terms, ((0, -terms.shape[0] % 16), (0, 0)))
    xg = lax.all_gather(after(jnp.concatenate([hidden, terms], axis=0), early[0]), "row", axis=0, tiled=True)
    xg = xg.reshape(n_row, -1, fw)
    count = norm_parameters.shape[0]
    norms = xg[:, tokens : tokens + 3 * count].astype(F32)
    norms = norms[:, :count] + norms[:, count : 2 * count] + norms[:, 2 * count :]
    last = last.reshape(n_col * 3 * deep, cols)
    last = lax.all_gather(last, "row", axis=0, tiled=True).reshape(n_row, n_col, 3, deep, cols)
    ff = channel_mix_shards.shape[2] // n_row
    late = channel_mix_shards.astype(BF16).reshape(2, deep, n_row, ff).transpose(2, 0, 1, 3)
    late = relay(after(late, early[0]))
    key, value = after(late[:, 0], early[-1]), after(late[:, 1], early[-1])
    keys = [key, ring(key)]
    key_last = back(key)

    prompts = tokens // LMAX
    lens = lax.dynamic_slice_in_dim(lengths, col * prompts, prompts, 0)
    shift = token_shift_weights.reshape(-1, n_row, fw).transpose(1, 0, 2)
    up = lax.dynamic_slice_in_dim(lowrank_up, row * hc, hc, 2)
    co = lax.dynamic_slice_in_dim(attention_coefficients, row * hc, hc, 1)
    even, odd, own, states = time_mix(
        place, lens, xg, norms, shift, lowrank_down, up, co, early, (key,), 2
    )

    keys[1] = after(keys[1], odd)
    for k in range(2, n_col - 1):
        keys.append(ring(keys[-1]))
    keys.append(key_last)
    other = to_row(after(odd, keys[1], key_last), 1)
    near = [(even[k].astype(F32) + other[k].astype(F32)).astype(BF16) for k in range(chips)]
    value = after(value, near[0])
    values = [value, ring(value)]
    value_last = back(value)
    pieces = [near[0]] + [to_row(near[k], 2 * k) for k in range(1, chips)]
    gains = norms.transpose(1, 0, 2).reshape(-1, width)
    mid, second, channel_in = settle(
        place, [pieces], own, jnp.concatenate([gains[2:4], token_shift_weights[5:6]], axis=0), 1
    )
    if chunk % LMAX:
        pairs = [(row_of(n), row_of(n + 1)) for n in range(n_row - 1)]
        edge = lax.ppermute(second[-1:], "row", pairs).astype(F32)
        edge = jnp.where(chunk_of(row) * chunk % LMAX == 0, 0.0, edge)
        wide = second.astype(F32)
        moved_on = jnp.concatenate([edge, wide[:-1]], axis=0)
        channel_in = (wide + (moved_on - wide) * token_shift_weights[5]).astype(BF16)
    values[1] = after(values[1], mid)
    for k in range(2, n_col - 1):
        values.append(ring(values[-1]))
    values.insert(n_col - 2, value_last)
    rows_in = [channel_in] + [to_row(channel_in, 2 * k) for k in range(1, chips)]
    rows_in = [piece for x in rows_in for piece in (x, to_row(x, 1))]
    act = key_products(place, rows_in, keys, (last,))
    pieces = []
    for group in (values[:-1], values[-1:]):
        even, low, high = value_products(n_row, act, group, pieces[0][1:] if pieces else ())
        other = [half[k] for half in (to_row(low, 1), to_row(high, 1)) for k in range(chips // 2)]
        near = [(even[k].astype(F32) + other[k].astype(F32)).astype(BF16) for k in range(chips)]
        pieces.append([near[0]] + [to_row(near[k], 2 * k) for k in range(1, chips)])
    out_own, third, _ = settle(
        place, pieces, mid, jnp.concatenate([gains[4:6], token_shift_weights[5:6]], axis=0), n_col
    )
    half = prompts // 2
    share = n_row // n_col
    states = after(states, values[-1]).reshape(2, half, states.shape[1], HEAD, HEAD)
    moved = []
    for j in range(2):
        pairs = []
        for r in range(n_row):
            for c in range(n_col):
                h = (r % 2) ^ j
                pairs.append((r * n_col + c, (2 * c + h) * n_col + r // share))
        piece = lax.dynamic_index_in_dim(states, (row % 2) ^ j, 0, keepdims=False)
        moved.append(lax.ppermute(piece, ("row", "col"), pairs))
    settled = jnp.take(jnp.stack(moved), (row % 2) ^ jnp.arange(2), axis=0)
    final_state = settled.transpose(1, 0, 2, 3, 4).reshape(half, -1, HEAD * HEAD).astype(F32)

    arrived = []
    for j in range(n_col):
        pairs = []
        for r in range(n_row):
            for c in range(n_col):
                pairs.append((r * n_col + c, (2 * c + r % 2) * n_col + ((r // 2) ^ j ^ (r % 2 * (n_col // 2)))))
        arrived.append(lax.ppermute(third, ("row", "col"), pairs))
    blocks = relay(out_own.reshape(chunk, n_row, fw).transpose(1, 0, 2))
    out_hidden = blocks.reshape(chips, 2, chunk, fw).transpose(1, 0, 2, 3).reshape(tokens, fw)
    next_rkv = next_products(place, arrived, token_shift_weights[6:9], last)
    return (out_hidden, next_rkv, final_state)


def solution(mesh):
    return jax.shard_map(
        per_device,
        mesh=mesh,
        in_specs=(
            P("col", "row"),
            P(),
            P(None, ("row", "col"), None),
            P(None, ("row", "col"), None),
            P(),
            P(),
            P(),
            P(),
            P(None, "row"),
        ),
        out_specs=(P("col", "row"), P(None, "row", "col"), P("row", "col", None)),
        check_vma=False,
    )
```

```python
import functools

import jax
import jax.numpy as jnp
from jax import lax
from jax.experimental import pallas as pl
from jax.experimental.pallas import tpu as pltpu
from jax.sharding import PartitionSpec as P

LMAX = 128
HEAD = 64
F32 = jnp.float32
BF16 = jnp.bfloat16


def bdot(a, b, ca=1, cb=0):
    return lax.dot_general(
        a.astype(BF16), b.astype(BF16), (((ca,), (cb,)), ((), ())), preferred_element_type=F32
    )


def halves(x):
    top = x.astype(BF16)
    return top, (x - top.astype(F32)).astype(BF16)


def dot3(a, b, ca=1, cb=0):
    ah, al = halves(a)
    bh, bl = halves(b)
    return bdot(ah, bh, ca, cb) + (bdot(ah, bl, ca, cb) + bdot(al, bh, ca, cb))


def head_sums(x, same):
    top, low = halves(x)
    return bdot(top, same) + bdot(low, same)


def time_kernel(nc, per, place_ref, lens, xg, norms, shift, ld, lu, co, *refs):
    wt = refs[:nc]
    even, odd, own, state_ref, mixes, w, sems = refs[-7:]
    rows = per * LMAX
    nb, _, fw = xg.shape
    width = nb * fw
    hc = w.shape[-1]
    chunk = even.shape[1]
    row, col = place_ref[0], place_ref[1]

    @pl.when(pl.program_id(0) == 0)
    def _():
        copies = [
            pltpu.make_async_copy(wt[k].at[:, m], w.at[m, :, (col + nc - k) % nc], sems.at[m, k])
            for m in range(4)
            for k in range(nc)
        ]
        for copy in copies:
            copy.start()
        for copy in copies:
            copy.wait()

    weight = [w[m].reshape(width, hc) for m in range(4)]
    blocks = [xg[i].astype(F32) for i in range(nb)]
    total = sum(jnp.sum(b, axis=1, keepdims=True) for b in blocks)
    square = sum(jnp.sum(b * b, axis=1, keepdims=True) for b in blocks)
    center = total / width
    scale = lax.rsqrt(square / width - center * center + 1e-05)
    first_row = lax.broadcasted_iota(jnp.int32, (rows, fw), 0) % LMAX == 0
    for i in range(nb):
        z = (xg[i].astype(F32) - center) * scale * norms[i, 0:1] + norms[i, 1:2]
        z = z.astype(BF16).astype(F32)
        step = jnp.where(first_row, 0.0, pltpu.roll(z, 1, 0)) - z
        for j in range(5):
            mixes[j, :, i * fw : (i + 1) * fw] = (z + step * shift[i, j : j + 1]).astype(BF16)
    r = bdot(mixes[0], weight[0])
    k = bdot(mixes[1], weight[1])
    v = bdot(mixes[2], weight[2])
    dl = bdot(mixes[3], ld[0])
    al = bdot(mixes[4], ld[1])
    logd = -0.606531 * jax.nn.sigmoid(co[0:1] + bdot(jnp.tanh(dl), lu[0]))
    rate = jax.nn.sigmoid(co[1:2] + bdot(al, lu[1]))
    lane_a = lax.broadcasted_iota(jnp.int32, (hc, hc), 0) // HEAD
    lane_b = lax.broadcasted_iota(jnp.int32, (hc, hc), 1) // HEAD
    same = (lane_a == lane_b).astype(BF16)
    kappa = k * co[2:3]
    kappa = kappa * lax.rsqrt(head_sums(kappa * kappa, same) + 1e-05)
    t_of = lax.broadcasted_iota(jnp.int32, (LMAX, LMAX), 0)
    u_of = lax.broadcasted_iota(jnp.int32, (LMAX, LMAX), 1)
    upto = u_of <= t_of
    before = u_of < t_of
    lower = upto.astype(BF16)
    low_lane = u_of < HEAD
    side = jnp.concatenate([low_lane, low_lane], axis=0)
    levels = [((t_of >> n) == (u_of >> n) + 1) & (((t_of >> n) & 1) == 1) for n in range(7)]
    eye = (t_of == u_of).astype(F32)
    place = lax.broadcasted_iota(jnp.int32, (LMAX, hc), 0)
    chains = []
    keep = []
    for p in range(per):
        at = slice(p * LMAX, (p + 1) * LMAX)
        live = (place < lens[pl.program_id(0) * per + p]).astype(F32)
        rp, kp, vp = r[at], k[at] * live, v[at] * live
        dp = logd[at] * live
        kh = kappa[at] * live
        wr = kh * rate[at]
        d1 = dp.astype(BF16)
        d2, d3 = halves(dp - d1.astype(F32))
        cum = bdot(lower, d1) + (bdot(lower, d2) + bdot(lower, d3))
        last = cum[LMAX - 1 : LMAX]
        mid = 0.5 * last
        grow = jnp.exp(mid - cum)
        tail = jnp.exp(last - mid)
        pull = -kh * jnp.exp(cum - dp - mid)
        read = rp * jnp.exp(cum - mid)
        wb = wr * grow
        kb = kp * grow
        keep.append((live, head_sums(rp * kp * co[3:4], same) * vp))
        for q in range(hc // 128):
            ln = slice(q * 128, (q + 1) * 128)
            right = jnp.concatenate([wb[:, ln], kb[:, ln]], axis=0)
            left = jnp.concatenate([pull[:, ln], read[:, ln]], axis=0)
            pair = []
            for h in range(2):
                g = bdot(jnp.where(side == (h == 0), left, 0.0), right, 1, 1)
                pair.append(
                    (
                        jnp.where(before, g[:LMAX, :LMAX], 0.0),
                        jnp.where(before, g[:LMAX, LMAX:], 0.0),
                        jnp.where(upto, g[LMAX:, :LMAX], 0.0),
                        jnp.where(upto, g[LMAX:, LMAX:], 0.0),
                    )
                )
            chains.append((p, q, pair, vp[:, ln], wb[:, ln] * tail[:, ln], kb[:, ln] * tail[:, ln]))
    strict = [c[2][h][0] for c in chains for h in range(2)]
    inverse = [eye + jnp.where(levels[0], a, 0.0) for a in strict]
    for n in range(1, 7):
        inner = [dot3(jnp.where(levels[n], a, 0.0), t) for a, t in zip(strict, inverse)]
        inverse = [t + dot3(t, m) for t, m in zip(inverse, inner)]
    outs = {}
    for i, (p, q, pair, vq, wt, kt) in enumerate(chains):
        us, ys = [], []
        for h in range(2):
            _, b, rw, rk = pair[h]
            u = dot3(inverse[2 * i + h], bdot(b, vq))
            us.append(u)
            ys.append(bdot(jnp.concatenate([rw, rk], axis=1), jnp.concatenate([u, vq], axis=0)))
        u = jnp.where(low_lane, us[0], us[1])
        outs[p, q] = jnp.where(low_lane, ys[0], ys[1])
        final = bdot(jnp.concatenate([u, vq], axis=0), jnp.concatenate([wt, kt], axis=0), 0, 0)
        state_ref[p, 2 * q] = final[:HEAD, :HEAD].astype(BF16)
        state_ref[p, 2 * q + 1] = final[HEAD:, HEAD:].astype(BF16)
    atts = []
    for p in range(per):
        live, extra = keep[p]
        y = jnp.concatenate([outs[p, q] for q in range(hc // 128)], axis=1)
        y = (y + extra) * live
        y = y - head_sums(y, same) / HEAD
        spread = head_sums(y * y, same) / HEAD
        atts.append((y * lax.rsqrt(spread + 0.00064) * co[4:5] + co[5:6]).astype(BF16))
    partial = bdot(jnp.concatenate(atts, axis=0), weight[3], 1, 1).astype(BF16)
    pieces = rows // chunk
    for t in range(pieces):
        n = pl.program_id(0) * pieces + t
        to = row ^ ((n % (nb // 2)) * 2 + n // (nb // 2))
        here = slice(t * chunk, (t + 1) * chunk)

        @pl.when(to == 0)
        def _():
            for i in range(nb):
                own[:, i * fw : (i + 1) * fw] = xg[i, here]

        @pl.when(to % 2 == 0)
        def _():
            even[to // 2] = partial[here]

        @pl.when(to % 2 == 1)
        def _():
            odd[to // 2] = partial[here]


def time_mix(place, lens, xg, norms, shift, ld, lu, co, wt, extra, per):
    nb, _, fw = xg.shape
    nc = len(wt)
    _, _, deep, hc = wt[0].shape
    prompts = lens.shape[0]
    tokens = prompts * LMAX
    width, chunk = nb * fw, tokens // nb

    def full(a):
        return pl.BlockSpec(a.shape, lambda i: (0,) * a.ndim)

    whole = pl.BlockSpec((nb // 2, chunk, width), lambda i: (0, 0, 0))
    rest = (norms, shift, ld, lu, co)
    return pl.pallas_call(
        functools.partial(time_kernel, nc, per),
        grid=(prompts // per,),
        in_specs=[pl.BlockSpec(memory_space=pltpu.SMEM)] * 2
        + [pl.BlockSpec((nb, per * LMAX, fw), lambda i: (0, i, 0))]
        + [full(a) for a in rest]
        + [pl.BlockSpec(memory_space=pl.ANY)] * (nc + len(extra)),
        out_specs=[
            whole,
            whole,
            pl.BlockSpec((chunk, width), lambda i: (0, 0)),
            pl.BlockSpec((per, hc // HEAD, HEAD, HEAD), lambda i: (i, 0, 0, 0)),
        ],
        out_shape=[
            jax.ShapeDtypeStruct((nb // 2, chunk, width), BF16),
            jax.ShapeDtypeStruct((nb // 2, chunk, width), BF16),
            jax.ShapeDtypeStruct((chunk, width), BF16),
            jax.ShapeDtypeStruct((prompts, hc // HEAD, HEAD, HEAD), BF16),
        ],
        scratch_shapes=[
            pltpu.VMEM((5, per * LMAX, width), BF16),
            pltpu.VMEM((4, nb, nc, deep, hc), BF16),
            pltpu.SemaphoreType.DMA((4, nc)),
        ],
        compiler_params=pltpu.CompilerParams(vmem_limit_bytes=50 * 2**20),
        cost_estimate=pl.CostEstimate(flops=40 * 10**9, bytes_accessed=2**24, transcendentals=0),
    )(place, lens, xg, *rest, *wt, *extra)


def shifted_mix(z, weight):
    first_row = lax.broadcasted_iota(jnp.int32, z.shape, 0) % LMAX == 0
    return (z + (jnp.where(first_row, 0.0, pltpu.roll(z, 1, 0)) - z) * weight).astype(BF16)


def settle_kernel(count, groups, quarters, place_ref, *refs):
    pieces = refs[: count * groups]
    base, gains, out, normal, blend = refs[count * groups : count * groups + 5]
    sums = []
    for g in range(groups):
        total = pieces[g * count][...].astype(F32)
        for piece in pieces[g * count + 1 : (g + 1) * count]:
            total = total + piece[...].astype(F32)
        sums.append(total)
    width = base.shape[1]
    if quarters == 1:
        added = sums[0]
    else:
        share = width // quarters
        sums = jnp.concatenate(sums, axis=1)
        sums = [sums[:, i : i + share] for i in range(0, width, share)]
        held = refs[-1]
        order = list(range(quarters - 2)) + [quarters - 1, quarters - 2]
        for q in range(quarters):
            held[(place_ref[1] + quarters - order[q]) % quarters] = sums[q]
        deep = sums[0].shape[1] // (2 * count)
        added = jnp.concatenate(
            [held[q, :, r * deep : (r + 1) * deep] for r in range(2 * count) for q in range(quarters)], axis=1
        )
    total = (base[...].astype(F32) + added).astype(BF16)
    out[...] = total
    z = total.astype(F32)
    center = jnp.sum(z, axis=1, keepdims=True) / width
    second = jnp.sum(z * z, axis=1, keepdims=True) / width
    z = (z - center) * lax.rsqrt(second - center * center + 1e-05) * gains[0:1] + gains[1:2]
    z = z.astype(BF16)
    normal[...] = z
    blend[...] = shifted_mix(z.astype(F32), gains[2:3])


def settle(place, pieces, base, gains, quarters):
    groups, count = len(pieces), len(pieces[0])
    flat = [piece for group in pieces for piece in group]
    spec = pl.BlockSpec(memory_space=pltpu.VMEM)
    held = [pltpu.VMEM((quarters, base.shape[0], base.shape[1] // quarters), F32)] if quarters > 1 else []
    return pl.pallas_call(
        functools.partial(settle_kernel, count, groups, quarters),
        in_specs=[pl.BlockSpec(memory_space=pltpu.SMEM)] + [spec] * (len(flat) + 2),
        out_specs=[spec] * 3,
        out_shape=[jax.ShapeDtypeStruct(base.shape, BF16)] * 3,
        scratch_shapes=held,
        compiler_params=pltpu.CompilerParams(vmem_limit_bytes=24 * 2**20),
        cost_estimate=pl.CostEstimate(flops=10**6, bytes_accessed=2**12, transcendentals=0),
    )(place, *flat, base, gains)


def after_kernel(*refs):
    pass


def after(x, *earlier):
    apart = pl.BlockSpec(memory_space=pl.ANY)
    return pl.pallas_call(
        after_kernel,
        in_specs=[apart] * (1 + len(earlier)),
        out_specs=apart,
        out_shape=jax.ShapeDtypeStruct(x.shape, x.dtype),
        input_output_aliases={0: 0},
    )(x, *earlier)


def key_kernel(nb, nc, place_ref, *refs):
    xs, shards = refs[:nb], refs[nb : nb + nc]
    act, x, w, sems = refs[-4:]
    col = place_ref[1]
    chunk, width = xs[0].shape
    moves = [pltpu.make_async_copy(xs[i], x.at[i], sems.at[nc + i]) for i in range(nb)]
    copies = [
        pltpu.make_async_copy(shards[k], w.at[:, (col + nc - k) % nc], sems.at[k]) for k in range(nc)
    ]
    for copy in copies + moves:
        copy.start()
    for copy in copies:
        copy.wait()
    weight = w[...].reshape(width, -1)
    for i in range(0, nb, 2):
        moves[i].wait()
        moves[i + 1].wait()
        pre = bdot(x[i : i + 2].reshape(2 * chunk, width), weight)
        act[i * chunk : (i + 2) * chunk, :] = jnp.square(jnp.maximum(pre, 0.0)).astype(BF16)


def key_products(place, xs, shards, extra):
    nb, nc = len(xs), len(shards)
    _, deep, ff = shards[0].shape
    chunk, width = xs[0].shape
    apart = pl.BlockSpec(memory_space=pl.ANY)
    return pl.pallas_call(
        functools.partial(key_kernel, nb, nc),
        in_specs=[pl.BlockSpec(memory_space=pltpu.SMEM)] + [apart] * (nb + nc + len(extra)),
        out_specs=pl.BlockSpec(memory_space=pltpu.VMEM),
        out_shape=jax.ShapeDtypeStruct((nb * chunk, ff), BF16),
        scratch_shapes=[
            pltpu.VMEM((nb, chunk, width), BF16),
            pltpu.VMEM((nb, nc, deep, ff), BF16),
            pltpu.SemaphoreType.DMA((nc + nb,)),
        ],
        compiler_params=pltpu.CompilerParams(vmem_limit_bytes=58 * 2**20),
        cost_estimate=pl.CostEstimate(flops=10**6, bytes_accessed=2**12, transcendentals=0),
    )(place, *xs, *shards, *extra)


def value_kernel(count, act, *refs):
    shards, (even, low, high) = refs[:count], refs[-3:]
    chips, chunk, _ = even.shape
    start = 0
    for q in range(count):
        weight = shards[q][...].reshape(-1, shards[q].shape[-1])
        at = slice(start, start + weight.shape[0])
        start += weight.shape[0]
        for k in range(chips):
            out = bdot(act[2 * k * chunk : (2 * k + 2) * chunk, :], weight, 1, 1).astype(BF16)
            even[k, :, at] = out[:chunk]
            odd = low if k < chips // 2 else high
            odd[k % (chips // 2), :, at] = out[chunk:]


def value_products(nb, act, shards, extra):
    deep = shards[0].shape[1]
    chunk = act.shape[0] // nb
    width = sum(x.shape[0] for x in shards) * deep
    spec = pl.BlockSpec(memory_space=pltpu.VMEM)
    return pl.pallas_call(
        functools.partial(value_kernel, len(shards)),
        in_specs=[spec] * (1 + len(shards)) + [pl.BlockSpec(memory_space=pl.ANY)] * len(extra),
        out_specs=[spec] * 3,
        out_shape=[jax.ShapeDtypeStruct((n, chunk, width), BF16) for n in (nb // 2, nb // 4, nb // 4)],
        compiler_params=pltpu.CompilerParams(vmem_limit_bytes=40 * 2**20),
        cost_estimate=pl.CostEstimate(flops=10**6, bytes_accessed=2**12, transcendentals=0),
    )(act, *shards, *extra)


def next_kernel(nc, place_ref, *refs):
    xs = refs[:nc]
    gate, given = refs[nc : nc + 2]
    out, x, w, sems = refs[-4:]
    col = place_ref[1]
    copies = [
        pltpu.make_async_copy(given.at[:, k, m], w.at[m, :, col ^ k], sems.at[m, k])
        for m in range(3)
        for k in range(nc)
    ]
    for copy in copies:
        copy.start()
    chunk, width = xs[0].shape
    for k in range(nc):
        at = col ^ k ^ (place_ref[0] % 2 * (nc // 2))
        x[pl.ds(pl.multiple_of(at * chunk, chunk), chunk), :] = xs[k][...]
    z = x[...].astype(F32)
    mixed = shifted_mix(z, gate[0:1])
    for copy in copies:
        copy.wait()
    for m in range(3):
        out[m] = bdot(mixed, w[m].reshape(width, -1)).astype(BF16)
        if m < 2:
            mixed = shifted_mix(z, gate[m + 1 : m + 2])


def next_products(place, xs, gate, given):
    nc = len(xs)
    chunk, width = xs[0].shape
    nb, _, _, deep, cols = given.shape
    spec = pl.BlockSpec(memory_space=pltpu.VMEM)
    return pl.pallas_call(
        functools.partial(next_kernel, nc),
        in_specs=[pl.BlockSpec(memory_space=pltpu.SMEM)]
        + [spec] * (nc + 1)
        + [pl.BlockSpec(memory_space=pl.ANY)],
        out_specs=spec,
        out_shape=jax.ShapeDtypeStruct((3, nc * chunk, cols), BF16),
        scratch_shapes=[
            pltpu.VMEM((nc * chunk, width), BF16),
            pltpu.VMEM((3, nb, nc, deep, cols), BF16),
            pltpu.SemaphoreType.DMA((3, nc)),
        ],
        compiler_params=pltpu.CompilerParams(vmem_limit_bytes=50 * 2**20),
        cost_estimate=pl.CostEstimate(flops=10**6, bytes_accessed=2**12, transcendentals=0),
    )(place, *xs, gate, given)


def state_kernel(place_ref, a, b, out):
    even = place_ref[0] % 2 == 0
    a, b = a[...].astype(F32), b[...].astype(F32)
    x = jnp.concatenate([jnp.where(even, a, b), jnp.where(even, b, a)], axis=1)
    for v in range(0, HEAD, 2):
        out[:, :, v * HEAD : (v + 2) * HEAD] = jnp.concatenate([x[:, :, v, :], x[:, :, v + 1, :]], axis=2)


def state_rows(place, a, b):
    spec = pl.BlockSpec(memory_space=pltpu.VMEM)
    return pl.pallas_call(
        state_kernel,
        in_specs=[pl.BlockSpec(memory_space=pltpu.SMEM), spec, spec],
        out_specs=spec,
        out_shape=jax.ShapeDtypeStruct((a.shape[0], 2 * a.shape[1], HEAD * HEAD), F32),
        compiler_params=pltpu.CompilerParams(vmem_limit_bytes=24 * 2**20),
        cost_estimate=pl.CostEstimate(flops=10**6, bytes_accessed=2**12, transcendentals=0),
    )(place, a, b)


def per_device(
    hidden,
    lengths,
    square_matrix_shards,
    channel_mix_shards,
    lowrank_down,
    lowrank_up,
    token_shift_weights,
    attention_coefficients,
    norm_parameters,
):
    n_row = lax.axis_size("row")
    n_col = lax.axis_size("col")
    row = lax.axis_index("row")
    col = lax.axis_index("col")
    chips = n_row // 2
    tokens, fw = hidden.shape
    width = token_shift_weights.shape[1]
    chunk = tokens // n_row
    deep = square_matrix_shards.shape[1]
    hc = width // n_row
    place = jnp.stack([row, col]).astype(jnp.int32)

    def to_row(x, k):
        return lax.ppermute(x, "row", [(i, i ^ k) for i in range(n_row)])

    def to_col(x, k):
        return lax.ppermute(x, "col", [(i, i ^ k) for i in range(n_col)])

    def chunk_of(r):
        return (r % 2) * chips + r // 2

    def row_of(n):
        return (n % chips) * 2 + n // chips

    def gather_row(x):
        mine = [x] + [to_row(x, 2 * k) for k in range(1, chips)]
        return [piece for m in mine for piece in (m, to_row(m, 1))]

    def ring(x):
        return lax.ppermute(x, "col", [(i, (i + 1) % n_col) for i in range(n_col)])

    def back(x):
        return lax.ppermute(x, "col", [(i, (i - 1) % n_col) for i in range(n_col)])

    def relay(x):
        return lax.all_to_all(x, "row", 0, 0, tiled=True)

    moving = square_matrix_shards[0:4].astype(BF16).reshape(4, deep, n_row, hc).transpose(2, 0, 1, 3)
    early = [relay(moving)]
    cols = width // n_col
    sent = [
        lax.dynamic_slice_in_dim(square_matrix_shards[4:7], (col ^ k) * cols, cols, 2).astype(BF16)
        for k in range(n_col)
    ]
    last = jnp.stack([sent[0]] + [to_col(sent[k], k) for k in range(1, n_col)])
    early[0] = after(early[0], last)
    for k in range(1, n_col):
        early.append(ring(early[-1]))
    top = lax.reduce_precision(norm_parameters, 8, 7)
    middle = lax.reduce_precision(norm_parameters - top, 8, 7)
    terms = jnp.concatenate([top, middle, norm_parameters - top - middle], axis=0).astype(BF16)
    terms = jnp.pad(terms, ((0, -terms.shape[0] % 16), (0, 0)))
    xg = lax.all_gather(after(jnp.concatenate([hidden, terms], axis=0), early[0]), "row", axis=0, tiled=True)
    xg = xg.reshape(n_row, -1, fw)
    count = norm_parameters.shape[0]
    norms = xg[:, tokens : tokens + 3 * count].astype(F32)
    norms = norms[:, :count] + norms[:, count : 2 * count] + norms[:, 2 * count :]
    last = last.reshape(n_col * 3 * deep, cols)
    last = lax.all_gather(last, "row", axis=0, tiled=True).reshape(n_row, n_col, 3, deep, cols)
    ff = channel_mix_shards.shape[2] // n_row
    late = channel_mix_shards.astype(BF16).reshape(2, deep, n_row, ff).transpose(2, 0, 1, 3)
    late = relay(after(late, early[0]))
    key, value = after(late[:, 0], early[-1]), after(late[:, 1], early[-1])
    keys = [key, ring(key)]
    key_last = back(key)

    prompts = tokens // LMAX
    lens = lax.dynamic_slice_in_dim(lengths, col * prompts, prompts, 0)
    shift = token_shift_weights.reshape(-1, n_row, fw).transpose(1, 0, 2)
    up = lax.dynamic_slice_in_dim(lowrank_up, row * hc, hc, 2)
    co = lax.dynamic_slice_in_dim(attention_coefficients, row * hc, hc, 1)
    even, odd, own, states = time_mix(
        place, lens, xg, norms, shift, lowrank_down, up, co, early, (key,), 2
    )

    keys[1] = after(keys[1], odd)
    for k in range(2, n_col - 1):
        keys.append(ring(keys[-1]))
    keys.append(key_last)
    other = to_row(after(odd, keys[1], key_last), 1)
    near = [(even[k].astype(F32) + other[k].astype(F32)).astype(BF16) for k in range(chips)]
    value = after(value, near[0])
    values = [value, ring(value)]
    value_last = back(value)
    pieces = [near[0]] + [to_row(near[k], 2 * k) for k in range(1, chips)]
    gains = norms.transpose(1, 0, 2).reshape(-1, width)
    mid, second, channel_in = settle(
        place, [pieces], own, jnp.concatenate([gains[2:4], token_shift_weights[5:6]], axis=0), 1
    )
    if chunk % LMAX:
        pairs = [(row_of(n), row_of(n + 1)) for n in range(n_row - 1)]
        edge = lax.ppermute(second[-1:], "row", pairs).astype(F32)
        edge = jnp.where(chunk_of(row) * chunk % LMAX == 0, 0.0, edge)
        wide = second.astype(F32)
        moved_on = jnp.concatenate([edge, wide[:-1]], axis=0)
        channel_in = (wide + (moved_on - wide) * token_shift_weights[5]).astype(BF16)
    values[1] = after(values[1], mid)
    for k in range(2, n_col - 1):
        values.append(ring(values[-1]))
    values.insert(n_col - 2, value_last)
    rows_in = [channel_in] + [to_row(channel_in, 2 * k) for k in range(1, chips)]
    rows_in = [piece for x in rows_in for piece in (x, to_row(x, 1))]
    act = key_products(place, rows_in, keys, (last,))
    pieces = []
    for group in (values[:-1], values[-1:]):
        even, low, high = value_products(n_row, act, group, pieces[0][1:] if pieces else ())
        other = [half[k] for half in (to_row(low, 1), to_row(high, 1)) for k in range(chips // 2)]
        near = [(even[k].astype(F32) + other[k].astype(F32)).astype(BF16) for k in range(chips)]
        pieces.append([near[0]] + [to_row(near[k], 2 * k) for k in range(1, chips)])
    out_own, third, _ = settle(
        place, pieces, mid, jnp.concatenate([gains[4:6], token_shift_weights[5:6]], axis=0), n_col
    )
    arrived = []
    for j in range(n_col):
        pairs = []
        for r in range(n_row):
            for c in range(n_col):
                pairs.append((r * n_col + c, (2 * c + r % 2) * n_col + ((r // 2) ^ j ^ (r % 2 * (n_col // 2)))))
        arrived.append(lax.ppermute(third, ("row", "col"), pairs))
    blocks = relay(out_own.reshape(chunk, n_row, fw).transpose(1, 0, 2))
    out_hidden = blocks.reshape(chips, 2, chunk, fw).transpose(1, 0, 2, 3).reshape(tokens, fw)
    half = prompts // 2
    share = n_row // n_col
    states = after(states, arrived[-1]).reshape(2, half, states.shape[1], HEAD, HEAD)
    moved = []
    for j in range(2):
        pairs = []
        for r in range(n_row):
            for c in range(n_col):
                h = (r % 2) ^ j
                pairs.append((r * n_col + c, (2 * c + h) * n_col + r // share))
        piece = lax.dynamic_index_in_dim(states, (row % 2) ^ j, 0, keepdims=False)
        moved.append(lax.ppermute(piece, ("row", "col"), pairs))
    final_state = state_rows(place, *moved)
    next_rkv = next_products(place, arrived, token_shift_weights[6:9], last)
    return (out_hidden, next_rkv, final_state)


def solution(mesh):
    return jax.shard_map(
        per_device,
        mesh=mesh,
        in_specs=(
            P("col", "row"),
            P(),
            P(None, ("row", "col"), None),
            P(None, ("row", "col"), None),
            P(),
            P(),
            P(),
            P(),
            P(None, "row"),
        ),
        out_specs=(P("col", "row"), P(None, "row", "col"), P("row", "col", None)),
        check_vma=False,
    )
```

```python
import functools

import jax
import jax.numpy as jnp
from jax import lax
from jax.experimental import pallas as pl
from jax.experimental.pallas import tpu as pltpu
from jax.sharding import PartitionSpec as P

LMAX = 128
HEAD = 64
F32 = jnp.float32
BF16 = jnp.bfloat16


def bdot(a, b, ca=1, cb=0):
    return lax.dot_general(
        a.astype(BF16), b.astype(BF16), (((ca,), (cb,)), ((), ())), preferred_element_type=F32
    )


def halves(x):
    top = x.astype(BF16)
    return top, (x - top.astype(F32)).astype(BF16)


def dot3(a, b, ca=1, cb=0):
    ah, al = halves(a)
    bh, bl = halves(b)
    return bdot(ah, bh, ca, cb) + (bdot(ah, bl, ca, cb) + bdot(al, bh, ca, cb))


def head_sums(x, same):
    top, low = halves(x)
    return bdot(top, same) + bdot(low, same)


def time_kernel(nc, per, place_ref, lens, xg, norms, shift, ld, lu, co, *refs):
    wt = refs[:nc]
    even, odd, own, state_ref, mixes, w, sems = refs[-7:]
    rows = per * LMAX
    nb, _, fw = xg.shape
    width = nb * fw
    hc = w.shape[-1]
    chunk = even.shape[1]
    row, col = place_ref[0], place_ref[1]

    @pl.when(pl.program_id(0) == 0)
    def _():
        copies = [
            pltpu.make_async_copy(wt[k].at[:, m], w.at[m, :, (col + nc - k) % nc], sems.at[m, k])
            for m in range(4)
            for k in range(nc)
        ]
        for copy in copies:
            copy.start()
        for copy in copies:
            copy.wait()

    weight = [w[m].reshape(width, hc) for m in range(4)]
    blocks = [xg[i].astype(F32) for i in range(nb)]
    total = sum(jnp.sum(b, axis=1, keepdims=True) for b in blocks)
    square = sum(jnp.sum(b * b, axis=1, keepdims=True) for b in blocks)
    center = total / width
    scale = lax.rsqrt(square / width - center * center + 1e-05)
    first_row = lax.broadcasted_iota(jnp.int32, (rows, fw), 0) % LMAX == 0
    for i in range(nb):
        z = (xg[i].astype(F32) - center) * scale * norms[i, 0:1] + norms[i, 1:2]
        z = z.astype(BF16).astype(F32)
        step = jnp.where(first_row, 0.0, pltpu.roll(z, 1, 0)) - z
        for j in range(5):
            mixes[j, :, i * fw : (i + 1) * fw] = (z + step * shift[i, j : j + 1]).astype(BF16)
    r = bdot(mixes[0], weight[0])
    k = bdot(mixes[1], weight[1])
    v = bdot(mixes[2], weight[2])
    dl = bdot(mixes[3], ld[0])
    al = bdot(mixes[4], ld[1])
    logd = -0.606531 * jax.nn.sigmoid(co[0:1] + bdot(jnp.tanh(dl), lu[0]))
    rate = jax.nn.sigmoid(co[1:2] + bdot(al, lu[1]))
    lane_a = lax.broadcasted_iota(jnp.int32, (hc, hc), 0) // HEAD
    lane_b = lax.broadcasted_iota(jnp.int32, (hc, hc), 1) // HEAD
    same = (lane_a == lane_b).astype(BF16)
    kappa = k * co[2:3]
    kappa = kappa * lax.rsqrt(head_sums(kappa * kappa, same) + 1e-05)
    t_of = lax.broadcasted_iota(jnp.int32, (LMAX, LMAX), 0)
    u_of = lax.broadcasted_iota(jnp.int32, (LMAX, LMAX), 1)
    upto = u_of <= t_of
    before = u_of < t_of
    lower = upto.astype(BF16)
    low_lane = u_of < HEAD
    side = jnp.concatenate([low_lane, low_lane], axis=0)
    levels = [((t_of >> n) == (u_of >> n) + 1) & (((t_of >> n) & 1) == 1) for n in range(7)]
    eye = (t_of == u_of).astype(F32)
    place = lax.broadcasted_iota(jnp.int32, (LMAX, hc), 0)
    chains = []
    keep = []
    for p in range(per):
        at = slice(p * LMAX, (p + 1) * LMAX)
        live = (place < lens[pl.program_id(0) * per + p]).astype(F32)
        rp, kp, vp = r[at], k[at] * live, v[at] * live
        dp = logd[at] * live
        kh = kappa[at] * live
        wr = kh * rate[at]
        d1 = dp.astype(BF16)
        d2, d3 = halves(dp - d1.astype(F32))
        cum = bdot(lower, d1) + (bdot(lower, d2) + bdot(lower, d3))
        last = cum[LMAX - 1 : LMAX]
        mid = 0.5 * last
        grow = jnp.exp(mid - cum)
        tail = jnp.exp(last - mid)
        pull = -kh * jnp.exp(cum - dp - mid)
        read = rp * jnp.exp(cum - mid)
        wb = wr * grow
        kb = kp * grow
        keep.append((live, head_sums(rp * kp * co[3:4], same) * vp))
        for q in range(hc // 128):
            ln = slice(q * 128, (q + 1) * 128)
            right = jnp.concatenate([wb[:, ln], kb[:, ln]], axis=0)
            left = jnp.concatenate([pull[:, ln], read[:, ln]], axis=0)
            pair = []
            for h in range(2):
                g = bdot(jnp.where(side == (h == 0), left, 0.0), right, 1, 1)
                pair.append(
                    (
                        jnp.where(before, g[:LMAX, :LMAX], 0.0),
                        jnp.where(before, g[:LMAX, LMAX:], 0.0),
                        jnp.where(upto, g[LMAX:, :LMAX], 0.0),
                        jnp.where(upto, g[LMAX:, LMAX:], 0.0),
                    )
                )
            chains.append((p, q, pair, vp[:, ln], wb[:, ln] * tail[:, ln], kb[:, ln] * tail[:, ln]))
    strict = [c[2][h][0] for c in chains for h in range(2)]
    inverse = [eye + jnp.where(levels[0], a, 0.0) for a in strict]
    for n in range(1, 7):
        inner = [dot3(jnp.where(levels[n], a, 0.0), t) for a, t in zip(strict, inverse)]
        inverse = [t + dot3(t, m) for t, m in zip(inverse, inner)]
    outs = {}
    for i, (p, q, pair, vq, wt, kt) in enumerate(chains):
        us, ys = [], []
        for h in range(2):
            _, b, rw, rk = pair[h]
            u = dot3(inverse[2 * i + h], bdot(b, vq))
            us.append(u)
            ys.append(bdot(jnp.concatenate([rw, rk], axis=1), jnp.concatenate([u, vq], axis=0)))
        u = jnp.where(low_lane, us[0], us[1])
        outs[p, q] = jnp.where(low_lane, ys[0], ys[1])
        final = bdot(jnp.concatenate([u, vq], axis=0), jnp.concatenate([wt, kt], axis=0), 0, 0)
        state_ref[p, 2 * q] = final[:HEAD, :HEAD].astype(BF16)
        state_ref[p, 2 * q + 1] = final[HEAD:, HEAD:].astype(BF16)
    atts = []
    for p in range(per):
        live, extra = keep[p]
        y = jnp.concatenate([outs[p, q] for q in range(hc // 128)], axis=1)
        y = (y + extra) * live
        y = y - head_sums(y, same) / HEAD
        spread = head_sums(y * y, same) / HEAD
        atts.append((y * lax.rsqrt(spread + 0.00064) * co[4:5] + co[5:6]).astype(BF16))
    partial = bdot(jnp.concatenate(atts, axis=0), weight[3], 1, 1).astype(BF16)
    pieces = rows // chunk
    for t in range(pieces):
        n = pl.program_id(0) * pieces + t
        to = row ^ ((n % (nb // 2)) * 2 + n // (nb // 2))
        here = slice(t * chunk, (t + 1) * chunk)

        @pl.when(to == 0)
        def _():
            for i in range(nb):
                own[:, i * fw : (i + 1) * fw] = xg[i, here]

        @pl.when(to % 2 == 0)
        def _():
            even[to // 2] = partial[here]

        @pl.when(to % 2 == 1)
        def _():
            odd[to // 2] = partial[here]


def time_mix(place, lens, xg, norms, shift, ld, lu, co, wt, extra, per):
    nb, _, fw = xg.shape
    nc = len(wt)
    _, _, deep, hc = wt[0].shape
    prompts = lens.shape[0]
    tokens = prompts * LMAX
    width, chunk = nb * fw, tokens // nb

    def full(a):
        return pl.BlockSpec(a.shape, lambda i: (0,) * a.ndim)

    whole = pl.BlockSpec((nb // 2, chunk, width), lambda i: (0, 0, 0))
    rest = (norms, shift, ld, lu, co)
    return pl.pallas_call(
        functools.partial(time_kernel, nc, per),
        grid=(prompts // per,),
        in_specs=[pl.BlockSpec(memory_space=pltpu.SMEM)] * 2
        + [pl.BlockSpec((nb, per * LMAX, fw), lambda i: (0, i, 0))]
        + [full(a) for a in rest]
        + [pl.BlockSpec(memory_space=pl.ANY)] * (nc + len(extra)),
        out_specs=[
            whole,
            whole,
            pl.BlockSpec((chunk, width), lambda i: (0, 0)),
            pl.BlockSpec((per, hc // HEAD, HEAD, HEAD), lambda i: (i, 0, 0, 0)),
        ],
        out_shape=[
            jax.ShapeDtypeStruct((nb // 2, chunk, width), BF16),
            jax.ShapeDtypeStruct((nb // 2, chunk, width), BF16),
            jax.ShapeDtypeStruct((chunk, width), BF16),
            jax.ShapeDtypeStruct((prompts, hc // HEAD, HEAD, HEAD), BF16),
        ],
        scratch_shapes=[
            pltpu.VMEM((5, per * LMAX, width), BF16),
            pltpu.VMEM((4, nb, nc, deep, hc), BF16),
            pltpu.SemaphoreType.DMA((4, nc)),
        ],
        compiler_params=pltpu.CompilerParams(vmem_limit_bytes=50 * 2**20),
        cost_estimate=pl.CostEstimate(flops=40 * 10**9, bytes_accessed=2**24, transcendentals=0),
    )(place, lens, xg, *rest, *wt, *extra)


def shifted_mix(z, weight):
    first_row = lax.broadcasted_iota(jnp.int32, z.shape, 0) % LMAX == 0
    return (z + (jnp.where(first_row, 0.0, pltpu.roll(z, 1, 0)) - z) * weight).astype(BF16)


def settle_kernel(count, groups, quarters, place_ref, *refs):
    pieces = refs[: count * groups]
    base, gains, out, normal, blend = refs[count * groups : count * groups + 5]
    sums = []
    for g in range(groups):
        total = pieces[g * count][...].astype(F32)
        for piece in pieces[g * count + 1 : (g + 1) * count]:
            total = total + piece[...].astype(F32)
        sums.append(total)
    width = base.shape[1]
    if quarters == 1:
        added = sums[0]
    else:
        share = width // quarters
        sums = jnp.concatenate(sums, axis=1)
        sums = [sums[:, i : i + share] for i in range(0, width, share)]
        held = refs[-1]
        order = list(range(quarters - 2)) + [quarters - 1, quarters - 2]
        for q in range(quarters):
            held[(place_ref[1] + quarters - order[q]) % quarters] = sums[q]
        deep = sums[0].shape[1] // (2 * count)
        added = jnp.concatenate(
            [held[q, :, r * deep : (r + 1) * deep] for r in range(2 * count) for q in range(quarters)], axis=1
        )
    total = (base[...].astype(F32) + added).astype(BF16)
    out[...] = total
    z = total.astype(F32)
    center = jnp.sum(z, axis=1, keepdims=True) / width
    second = jnp.sum(z * z, axis=1, keepdims=True) / width
    z = (z - center) * lax.rsqrt(second - center * center + 1e-05) * gains[0:1] + gains[1:2]
    z = z.astype(BF16)
    normal[...] = z
    blend[...] = shifted_mix(z.astype(F32), gains[2:3])


def settle(place, pieces, base, gains, quarters):
    groups, count = len(pieces), len(pieces[0])
    flat = [piece for group in pieces for piece in group]
    spec = pl.BlockSpec(memory_space=pltpu.VMEM)
    held = [pltpu.VMEM((quarters, base.shape[0], base.shape[1] // quarters), F32)] if quarters > 1 else []
    return pl.pallas_call(
        functools.partial(settle_kernel, count, groups, quarters),
        in_specs=[pl.BlockSpec(memory_space=pltpu.SMEM)] + [spec] * (len(flat) + 2),
        out_specs=[spec] * 3,
        out_shape=[jax.ShapeDtypeStruct(base.shape, BF16)] * 3,
        scratch_shapes=held,
        compiler_params=pltpu.CompilerParams(vmem_limit_bytes=24 * 2**20),
        cost_estimate=pl.CostEstimate(flops=10**6, bytes_accessed=2**12, transcendentals=0),
    )(place, *flat, base, gains)


def after_kernel(*refs):
    pass


def after(x, *earlier):
    apart = pl.BlockSpec(memory_space=pl.ANY)
    return pl.pallas_call(
        after_kernel,
        in_specs=[apart] * (1 + len(earlier)),
        out_specs=apart,
        out_shape=jax.ShapeDtypeStruct(x.shape, x.dtype),
        input_output_aliases={0: 0},
    )(x, *earlier)


def key_kernel(nb, nc, place_ref, *refs):
    xs, shards = refs[:nb], refs[nb : nb + nc]
    act, x, w, sems = refs[-4:]
    col = place_ref[1]
    chunk, width = xs[0].shape
    moves = [pltpu.make_async_copy(xs[i], x.at[i], sems.at[nc + i]) for i in range(nb)]
    copies = [
        pltpu.make_async_copy(shards[k], w.at[:, (col + nc - k) % nc], sems.at[k]) for k in range(nc)
    ]
    for copy in copies + moves:
        copy.start()
    for copy in copies:
        copy.wait()
    weight = w[...].reshape(width, -1)
    for i in range(0, nb, 2):
        moves[i].wait()
        moves[i + 1].wait()
        pre = bdot(x[i : i + 2].reshape(2 * chunk, width), weight)
        act[i * chunk : (i + 2) * chunk, :] = jnp.square(jnp.maximum(pre, 0.0)).astype(BF16)


def key_products(place, xs, shards, extra):
    nb, nc = len(xs), len(shards)
    _, deep, ff = shards[0].shape
    chunk, width = xs[0].shape
    apart = pl.BlockSpec(memory_space=pl.ANY)
    return pl.pallas_call(
        functools.partial(key_kernel, nb, nc),
        in_specs=[pl.BlockSpec(memory_space=pltpu.SMEM)] + [apart] * (nb + nc + len(extra)),
        out_specs=pl.BlockSpec(memory_space=pltpu.VMEM),
        out_shape=jax.ShapeDtypeStruct((nb * chunk, ff), BF16),
        scratch_shapes=[
            pltpu.VMEM((nb, chunk, width), BF16),
            pltpu.VMEM((nb, nc, deep, ff), BF16),
            pltpu.SemaphoreType.DMA((nc + nb,)),
        ],
        compiler_params=pltpu.CompilerParams(vmem_limit_bytes=40 * 2**20),
        cost_estimate=pl.CostEstimate(flops=10**6, bytes_accessed=2**12, transcendentals=0),
    )(place, *xs, *shards, *extra)


def value_kernel(count, act, *refs):
    shards, (even, low, high) = refs[:count], refs[-3:]
    chips, chunk, _ = even.shape
    start = 0
    for q in range(count):
        weight = shards[q][...].reshape(-1, shards[q].shape[-1])
        at = slice(start, start + weight.shape[0])
        start += weight.shape[0]
        for k in range(chips):
            out = bdot(act[2 * k * chunk : (2 * k + 2) * chunk, :], weight, 1, 1).astype(BF16)
            even[k, :, at] = out[:chunk]
            odd = low if k < chips // 2 else high
            odd[k % (chips // 2), :, at] = out[chunk:]


def value_products(nb, act, shards, extra):
    deep = shards[0].shape[1]
    chunk = act.shape[0] // nb
    width = sum(x.shape[0] for x in shards) * deep
    spec = pl.BlockSpec(memory_space=pltpu.VMEM)
    return pl.pallas_call(
        functools.partial(value_kernel, len(shards)),
        in_specs=[spec] * (1 + len(shards)) + [pl.BlockSpec(memory_space=pl.ANY)] * len(extra),
        out_specs=[spec] * 3,
        out_shape=[jax.ShapeDtypeStruct((n, chunk, width), BF16) for n in (nb // 2, nb // 4, nb // 4)],
        compiler_params=pltpu.CompilerParams(vmem_limit_bytes=40 * 2**20),
        cost_estimate=pl.CostEstimate(flops=10**6, bytes_accessed=2**12, transcendentals=0),
    )(act, *shards, *extra)


def next_kernel(nc, place_ref, *refs):
    xs = refs[:nc]
    gate, given = refs[nc : nc + 2]
    out, x, w, sems = refs[-4:]
    col = place_ref[1]
    copies = [
        pltpu.make_async_copy(given.at[:, k, m], w.at[m, :, col ^ k], sems.at[m, k])
        for m in range(3)
        for k in range(nc)
    ]
    for copy in copies:
        copy.start()
    chunk, width = xs[0].shape
    for k in range(nc):
        at = col ^ k ^ (place_ref[0] % 2 * (nc // 2))
        x[pl.ds(pl.multiple_of(at * chunk, chunk), chunk), :] = xs[k][...]
    z = x[...].astype(F32)
    mixed = shifted_mix(z, gate[0:1])
    for copy in copies:
        copy.wait()
    for m in range(3):
        out[m] = bdot(mixed, w[m].reshape(width, -1)).astype(BF16)
        if m < 2:
            mixed = shifted_mix(z, gate[m + 1 : m + 2])


def next_products(place, xs, gate, given):
    nc = len(xs)
    chunk, width = xs[0].shape
    nb, _, _, deep, cols = given.shape
    spec = pl.BlockSpec(memory_space=pltpu.VMEM)
    return pl.pallas_call(
        functools.partial(next_kernel, nc),
        in_specs=[pl.BlockSpec(memory_space=pltpu.SMEM)]
        + [spec] * (nc + 1)
        + [pl.BlockSpec(memory_space=pl.ANY)],
        out_specs=spec,
        out_shape=jax.ShapeDtypeStruct((3, nc * chunk, cols), BF16),
        scratch_shapes=[
            pltpu.VMEM((nc * chunk, width), BF16),
            pltpu.VMEM((3, nb, nc, deep, cols), BF16),
            pltpu.SemaphoreType.DMA((3, nc)),
        ],
        compiler_params=pltpu.CompilerParams(vmem_limit_bytes=50 * 2**20),
        cost_estimate=pl.CostEstimate(flops=10**6, bytes_accessed=2**12, transcendentals=0),
    )(place, *xs, gate, given)


def state_kernel(place_ref, a, b, out):
    even = place_ref[0] % 2 == 0
    a, b = a[...].astype(F32), b[...].astype(F32)
    x = jnp.concatenate([jnp.where(even, a, b), jnp.where(even, b, a)], axis=1)
    for v in range(0, HEAD, 2):
        out[:, :, v * HEAD : (v + 2) * HEAD] = jnp.concatenate([x[:, :, v, :], x[:, :, v + 1, :]], axis=2)


def state_rows(place, a, b):
    spec = pl.BlockSpec(memory_space=pltpu.VMEM)
    return pl.pallas_call(
        state_kernel,
        in_specs=[pl.BlockSpec(memory_space=pltpu.SMEM), spec, spec],
        out_specs=spec,
        out_shape=jax.ShapeDtypeStruct((a.shape[0], 2 * a.shape[1], HEAD * HEAD), F32),
        compiler_params=pltpu.CompilerParams(vmem_limit_bytes=24 * 2**20),
        cost_estimate=pl.CostEstimate(flops=10**6, bytes_accessed=2**12, transcendentals=0),
    )(place, a, b)


def per_device(
    hidden,
    lengths,
    square_matrix_shards,
    channel_mix_shards,
    lowrank_down,
    lowrank_up,
    token_shift_weights,
    attention_coefficients,
    norm_parameters,
):
    n_row = lax.axis_size("row")
    n_col = lax.axis_size("col")
    row = lax.axis_index("row")
    col = lax.axis_index("col")
    chips = n_row // 2
    tokens, fw = hidden.shape
    width = token_shift_weights.shape[1]
    chunk = tokens // n_row
    deep = square_matrix_shards.shape[1]
    hc = width // n_row
    place = jnp.stack([row, col]).astype(jnp.int32)

    def to_row(x, k):
        return lax.ppermute(x, "row", [(i, i ^ k) for i in range(n_row)])

    def to_col(x, k):
        return lax.ppermute(x, "col", [(i, i ^ k) for i in range(n_col)])

    def chunk_of(r):
        return (r % 2) * chips + r // 2

    def row_of(n):
        return (n % chips) * 2 + n // chips

    def gather_row(x):
        mine = [x] + [to_row(x, 2 * k) for k in range(1, chips)]
        return [piece for m in mine for piece in (m, to_row(m, 1))]

    def ring(x):
        return lax.ppermute(x, "col", [(i, (i + 1) % n_col) for i in range(n_col)])

    def back(x):
        return lax.ppermute(x, "col", [(i, (i - 1) % n_col) for i in range(n_col)])

    def relay(x):
        return lax.all_to_all(x, "row", 0, 0, tiled=True)

    moving = square_matrix_shards[0:4].astype(BF16).reshape(4, deep, n_row, hc).transpose(2, 0, 1, 3)
    early = [relay(moving)]
    cols = width // n_col
    sent = [
        lax.dynamic_slice_in_dim(square_matrix_shards[4:7], (col ^ k) * cols, cols, 2).astype(BF16)
        for k in range(n_col)
    ]
    last = jnp.stack([sent[0]] + [to_col(sent[k], k) for k in range(1, n_col)])
    early[0] = after(early[0], last)
    for k in range(1, n_col):
        early.append(ring(early[-1]))
    top = lax.reduce_precision(norm_parameters, 8, 7)
    middle = lax.reduce_precision(norm_parameters - top, 8, 7)
    terms = jnp.concatenate([top, middle, norm_parameters - top - middle], axis=0).astype(BF16)
    terms = jnp.pad(terms, ((0, -terms.shape[0] % 16), (0, 0)))
    xg = lax.all_gather(after(jnp.concatenate([hidden, terms], axis=0), early[0]), "row", axis=0, tiled=True)
    xg = xg.reshape(n_row, -1, fw)
    count = norm_parameters.shape[0]
    norms = xg[:, tokens : tokens + 3 * count].astype(F32)
    norms = norms[:, :count] + norms[:, count : 2 * count] + norms[:, 2 * count :]
    last = last.reshape(n_col * 3 * deep, cols)
    last = lax.all_gather(last, "row", axis=0, tiled=True).reshape(n_row, n_col, 3, deep, cols)
    ff = channel_mix_shards.shape[2] // n_row
    late = channel_mix_shards.astype(BF16).reshape(2, deep, n_row, ff).transpose(2, 0, 1, 3)
    late = relay(after(late, early[0]))
    key, value = after(late[:, 0], early[-1]), after(late[:, 1], early[-1])
    keys = [key, ring(key)]
    key_last = back(key)

    prompts = tokens // LMAX
    lens = lax.dynamic_slice_in_dim(lengths, col * prompts, prompts, 0)
    shift = token_shift_weights.reshape(-1, n_row, fw).transpose(1, 0, 2)
    up = lax.dynamic_slice_in_dim(lowrank_up, row * hc, hc, 2)
    co = lax.dynamic_slice_in_dim(attention_coefficients, row * hc, hc, 1)
    even, odd, own, states = time_mix(
        place, lens, xg, norms, shift, lowrank_down, up, co, early, (key,), 2
    )

    keys[1] = after(keys[1], odd)
    for k in range(2, n_col - 1):
        keys.append(ring(keys[-1]))
    keys.append(key_last)
    other = to_row(after(odd, keys[1], key_last), 1)
    near = [(even[k].astype(F32) + other[k].astype(F32)).astype(BF16) for k in range(chips)]
    value = after(value, near[0])
    values = [value, ring(value)]
    value_last = back(value)
    pieces = [near[0]] + [to_row(near[k], 2 * k) for k in range(1, chips)]
    gains = norms.transpose(1, 0, 2).reshape(-1, width)
    mid, second, channel_in = settle(
        place, [pieces], own, jnp.concatenate([gains[2:4], token_shift_weights[5:6]], axis=0), 1
    )
    if chunk % LMAX:
        pairs = [(row_of(n), row_of(n + 1)) for n in range(n_row - 1)]
        edge = lax.ppermute(second[-1:], "row", pairs).astype(F32)
        edge = jnp.where(chunk_of(row) * chunk % LMAX == 0, 0.0, edge)
        wide = second.astype(F32)
        moved_on = jnp.concatenate([edge, wide[:-1]], axis=0)
        channel_in = (wide + (moved_on - wide) * token_shift_weights[5]).astype(BF16)
    values[1] = after(values[1], mid)
    for k in range(2, n_col - 1):
        values.append(ring(values[-1]))
    values.insert(n_col - 2, value_last)
    rows_in = [channel_in] + [to_row(channel_in, 2 * k) for k in range(1, chips)]
    rows_in = [piece for x in rows_in for piece in (x, to_row(x, 1))]
    act = key_products(place, rows_in, keys, (last,))
    pieces = []
    for group in (values[:-1], values[-1:]):
        even, low, high = value_products(n_row, act, group, pieces[0][1:] if pieces else ())
        other = [half[k] for half in (to_row(low, 1), to_row(high, 1)) for k in range(chips // 2)]
        near = [(even[k].astype(F32) + other[k].astype(F32)).astype(BF16) for k in range(chips)]
        pieces.append([near[0]] + [to_row(near[k], 2 * k) for k in range(1, chips)])
    out_own, third, _ = settle(
        place, pieces, mid, jnp.concatenate([gains[4:6], token_shift_weights[5:6]], axis=0), n_col
    )
    arrived = []
    for j in range(n_col):
        pairs = []
        for r in range(n_row):
            for c in range(n_col):
                pairs.append((r * n_col + c, (2 * c + r % 2) * n_col + ((r // 2) ^ j ^ (r % 2 * (n_col // 2)))))
        arrived.append(lax.ppermute(third, ("row", "col"), pairs))
    blocks = relay(out_own.reshape(chunk, n_row, fw).transpose(1, 0, 2))
    out_hidden = blocks.reshape(chips, 2, chunk, fw).transpose(1, 0, 2, 3).reshape(tokens, fw)
    half = prompts // 2
    share = n_row // n_col
    states = after(states, arrived[2]).reshape(2, half, states.shape[1], HEAD, HEAD)
    moved = []
    for j in range(2):
        pairs = []
        for r in range(n_row):
            for c in range(n_col):
                h = (r % 2) ^ j
                pairs.append((r * n_col + c, (2 * c + h) * n_col + r // share))
        piece = lax.dynamic_index_in_dim(states, (row % 2) ^ j, 0, keepdims=False)
        moved.append(lax.ppermute(piece, ("row", "col"), pairs))
    final_state = state_rows(place, *moved)
    next_rkv = next_products(place, arrived, token_shift_weights[6:9], last)
    return (out_hidden, next_rkv, final_state)


def solution(mesh):
    return jax.shard_map(
        per_device,
        mesh=mesh,
        in_specs=(
            P("col", "row"),
            P(),
            P(None, ("row", "col"), None),
            P(None, ("row", "col"), None),
            P(),
            P(),
            P(),
            P(),
            P(None, "row"),
        ),
        out_specs=(P("col", "row"), P(None, "row", "col"), P("row", "col", None)),
        check_vma=False,
    )
```
